256 devices in a mesh: outer: 16 (over x, y), inner: 16 (over z, core).
Axes of the slice: x: 4, y: 4, z: 8, core: 2. Of those that a mesh axis runs over, the one named last changes fastest.
Arguments:
- queries: bfloat16 [32768, 1024], P(('outer', 'inner')), may hold values from -6 to 6
- keys: bfloat16 [32768, 1024], P(('outer', 'inner')), may hold values from -6 to 6
- values: bfloat16 [32768, 1024], P(('outer', 'inner')), may hold values from -6 to 6
- saved_out: bfloat16 [32768, 1024], P(('outer', 'inner')), may hold values from -6 to 6
- out_grad: bfloat16 [32768, 1024], P(('outer', 'inner')), may hold values from -6 to 6
- offsets: int32 [16], replicated, may hold values from 0 to 15
Outputs:
- queries_grad: bfloat16 [32768, 1024], P(('outer', 'inner'))
- keys_grad: bfloat16 [32768, 1024], P(('outer', 'inner'))
- values_grad: bfloat16 [32768, 1024], P(('outer', 'inner'))
The draws below stay inside these ranges and needn't reach their ends.
All inputs are finite; a program needn't handle non-finite values.
Results may differ from the reference program's by a relative error of at most 0.007.
Values may be sent and summed in bfloat16 or wider, within the bound.
No kernel may reach another device: no remote copies, remote signals or barrier semaphores. Data moves between devices by JAX's collectives and lax.ppermute only.
A program may use at most 128 MiB of HBM per device.

```python
import jax
import jax.numpy as jnp
from jax import lax

HEADS = 16
HD = 64
BLOCK = 128
SEGMENT = 2048
TOKENS = 32768
N_OUTER = 16


def draw_queries(key, part):
    key = jax.random.fold_in(key, 3)
    base = jnp.clip(jax.random.normal(key, (TOKENS, HEADS * HD), jnp.float32), -6.0, 6.0)
    return base.astype(jnp.bfloat16)


def draw_keys(key, part):
    key = jax.random.fold_in(key, 5)
    base = jnp.clip(jax.random.normal(key, (TOKENS, HEADS * HD), jnp.float32), -6.0, 6.0)
    return base.astype(jnp.bfloat16)


def set_ends(entries, own_key, smallest, largest):
    longest = entries.shape.index(max(entries.shape))
    spots = []
    for shift in (0, 1):
        where = [jax.random.randint(jax.random.fold_in(own_key, axis), (), 0, length) for axis, length in enumerate(entries.shape)]
        where[longest] = (where[longest] + shift) % entries.shape[longest]
        spots.append(tuple(where))
    return entries.at[spots[0]].set(smallest).at[spots[1]].set(largest)


def steps_of(rng, extent, cuts, smallest, top_value):
    factor_of, own = 1.0, jax.random.fold_in(rng, 6)
    for axis_at, shards_of in cuts:
        draws = jnp.exp(jax.random.uniform(jax.random.fold_in(own, axis_at), (shards_of,), jnp.float32, smallest / len(cuts), top_value / len(cuts)))
        factor_of = factor_of * jnp.repeat(draws, extent[axis_at] // shards_of).reshape([-1 if axis == axis_at else 1 for axis in range(len(extent))])
    return factor_of


def centred(rng, dims, width, most, pieces=(), kind=jnp.bfloat16):
    drawn = jax.random.normal(rng, dims, jnp.float32) * width
    if len(pieces) > 0:
        drawn = steps_of(rng, dims, pieces, -0.22, 0.18) * drawn
    return jnp.clip(drawn, min=-most, max=most).astype(kind)


def setup_inputs(seed: int = 0) -> dict:
    streams_of = jax.random.split(jax.random.key(seed), 7)
    queries = draw_queries(jax.random.fold_in(streams_of[6], 71), 0)
    keys = draw_keys(jax.random.fold_in(streams_of[6], 71), 0)
    values = centred(streams_of[2], (TOKENS, HEADS * HD), 1.0, 6.0, ((0, 256),))
    saved_out = centred(streams_of[3], (TOKENS, HEADS * HD), 1.0, 6.0, ((0, 256),))
    out_grad = centred(streams_of[4], (TOKENS, HEADS * HD), 1.0, 6.0, ((0, 256),))
    offsets = set_ends(jax.random.randint(streams_of[5], (HEADS,), 0, N_OUTER), jax.random.fold_in(streams_of[5], 1), 0, N_OUTER - 1).astype(jnp.int32)
    return dict(queries=queries, keys=keys, values=values, saved_out=saved_out, out_grad=out_grad, offsets=offsets)


def pick_rows(array, offset):
    shaped = array.reshape((-1, N_OUTER, BLOCK) + array.shape[1:])
    chosen = lax.dynamic_index_in_dim(shaped, offset, 1, keepdims=False)
    return chosen.reshape((-1,) + array.shape[1:])


def place_rows(rows_in, offset):
    shaped = rows_in.reshape((-1, 1, BLOCK) + rows_in.shape[1:])
    select = (jnp.arange(N_OUTER) == offset).reshape((1, N_OUTER, 1) + (1,) * (rows_in.ndim - 1))
    placed = jnp.where(select, shaped, jnp.zeros((), rows_in.dtype))
    return placed.reshape((-1,) + rows_in.shape[1:])


def head_grads(args):
    query_rows, key_rows, value_rows, saved_rows, grad_rows, offset = args
    scale = HD ** -0.5
    far_keys = pick_rows(key_rows, offset)
    far_values = pick_rows(value_rows, offset)
    row_term = jnp.sum(grad_rows.astype(jnp.float32) * saved_rows.astype(jnp.float32), axis=1)
    flags = ((jnp.arange(TOKENS) // BLOCK) % N_OUTER) == offset

    def segment(inner_args):
        seg_q, seg_k, seg_v, seg_g, seg_term, seg_flag = inner_args
        near = jnp.dot(seg_q, seg_k.T, preferred_element_type=jnp.float32) * scale
        far = jnp.dot(seg_q, far_keys.T, preferred_element_type=jnp.float32) * scale
        top_near = jnp.max(near, axis=1)
        top = jnp.where(seg_flag, jnp.maximum(top_near, jnp.max(far, axis=1)), top_near)
        near_sum = jnp.sum(jnp.exp(near - top[:, None]), axis=1)
        far_sum = jnp.where(seg_flag, jnp.sum(jnp.exp(far - top[:, None]), axis=1), jnp.float32(0.0))
        lse = top + jnp.log(near_sum + far_sum)
        prob_near = jnp.exp(near - lse[:, None])
        prob_far = jnp.where(seg_flag[:, None], jnp.exp(far - lse[:, None]), jnp.float32(0.0))
        dprob_near = jnp.dot(seg_g, seg_v.T, preferred_element_type=jnp.float32)
        dprob_far = jnp.dot(seg_g, far_values.T, preferred_element_type=jnp.float32)
        dscore_near = (prob_near * (dprob_near - seg_term[:, None])).astype(jnp.bfloat16)
        dscore_far = (prob_far * (dprob_far - seg_term[:, None])).astype(jnp.bfloat16)
        query_grad = (jnp.dot(dscore_near, seg_k, preferred_element_type=jnp.float32)
                      + jnp.dot(dscore_far, far_keys, preferred_element_type=jnp.float32)) * scale
        key_near = jnp.dot(dscore_near.T, seg_q, preferred_element_type=jnp.float32) * scale
        value_near = jnp.dot(prob_near.astype(jnp.bfloat16).T, seg_g, preferred_element_type=jnp.float32)
        key_far = jnp.dot(dscore_far.T, seg_q, preferred_element_type=jnp.float32) * scale
        value_far = jnp.dot(prob_far.astype(jnp.bfloat16).T, seg_g, preferred_element_type=jnp.float32)
        return query_grad, key_near, value_near, key_far, value_far

    def by_segment(array):
        return array.reshape((N_OUTER, SEGMENT) + array.shape[1:])

    results = lax.map(segment, (by_segment(query_rows), by_segment(key_rows), by_segment(value_rows),
                                by_segment(grad_rows), by_segment(row_term), by_segment(flags)))
    query_grad = results[0].reshape(TOKENS, HD)
    key_far = jnp.sum(results[3], axis=0)
    value_far = jnp.sum(results[4], axis=0)
    key_grad = results[1].reshape(TOKENS, HD) + place_rows(key_far, offset)
    value_grad = results[2].reshape(TOKENS, HD) + place_rows(value_far, offset)
    return query_grad.astype(jnp.bfloat16), key_grad.astype(jnp.bfloat16), value_grad.astype(jnp.bfloat16)


def reference(queries, keys, values, saved_out, out_grad, offsets):
    def split_heads(array):
        return array.reshape(TOKENS, HEADS, HD).transpose(1, 0, 2)

    def join_heads(array):
        return array.transpose(1, 0, 2).reshape(TOKENS, HEADS * HD)

    grads = lax.map(head_grads, (split_heads(queries), split_heads(keys), split_heads(values),
                                 split_heads(saved_out), split_heads(out_grad), offsets.astype(jnp.int32)))
    return join_heads(grads[0]), join_heads(grads[1]), join_heads(grads[2])
```

```python
import jax
import jax.numpy as jnp
from jax import lax
from jax.experimental import pallas as pl
from jax.experimental.pallas import tpu as pltpu
from jax.sharding import PartitionSpec as P

HEADS = 16
HD = 64
BLOCK = 128
NB = 16
SEG = NB * BLOCK
CHUNK = 256
BF = jnp.bfloat16
F32 = jnp.float32
VMEM = pl.BlockSpec(memory_space=pltpu.VMEM)
SMEM = pl.BlockSpec(memory_space=pltpu.SMEM)
QG_ROWS = BLOCK + 16
OUT_ROWS = BLOCK + HD


def params(mib):
    return pltpu.CompilerParams(vmem_limit_bytes=mib * 1024 * 1024)


def cost(flops, nbytes, exps=0):
    return pl.CostEstimate(flops=flops, bytes_accessed=nbytes, transcendentals=exps)


def dot(a, b):
    return jnp.dot(a, b, preferred_element_type=F32)


def dot_nt(a, b):
    return lax.dot_general(a, b, (((1,), (1,)), ((), ())), preferred_element_type=F32)


def split3(x):
    high = x.astype(BF)
    rest = x - high.astype(F32)
    mid = rest.astype(BF)
    low = (rest - mid.astype(F32)).astype(BF)
    return high, mid, low


def pack_kernel(q_ref, k_ref, v_ref, o_ref, g_ref, kv_ref, qg_ref):
    head_of = lax.broadcasted_iota(jnp.int32, (HEADS, HEADS * HD), 1) // HD
    mine = head_of == lax.broadcasted_iota(jnp.int32, (HEADS, HEADS * HD), 0)
    ones = jnp.where(mine, 1.0, 0.0).astype(BF)
    product = g_ref[...].astype(F32) * o_ref[...].astype(F32)
    high = product.astype(BF)
    low = (product - high.astype(F32)).astype(BF)
    terms = dot_nt(ones, high) + dot_nt(ones, low)
    parts = [part.astype(F32) for part in split3(terms)]
    row = lax.broadcasted_iota(jnp.int32, (16, BLOCK), 0)
    for pair in range(HEADS // 2):
        cols = slice(pair * 2 * HD, (pair + 1) * 2 * HD)
        q, k, v, g = (
            (q_ref[:, cols].astype(F32) * (HD**-0.5)).astype(BF),
            k_ref[:, cols],
            v_ref[:, cols],
            g_ref[:, cols],
        )
        for sub in range(2):
            head = 2 * pair + sub
            half = slice(sub * HD, (sub + 1) * HD)
            kv_ref[head] = jnp.concatenate([k[:, half], v[:, half]], axis=1)
            qg_ref[head, :BLOCK, :] = jnp.concatenate([q[:, half], g[:, half]], axis=1)
            tail = jnp.zeros((16, BLOCK), F32)
            for n, part in enumerate(parts):
                tail = jnp.where(row == n, part[head : head + 1, :], tail)
            qg_ref[head, BLOCK:, :] = tail.astype(BF)


def pack(queries, keys, values, saved_out, out_grad):
    return pl.pallas_call(
        pack_kernel,
        out_shape=(
            jax.ShapeDtypeStruct((HEADS, BLOCK, 2 * HD), BF),
            jax.ShapeDtypeStruct((HEADS, QG_ROWS, 2 * HD), BF),
        ),
        in_specs=[VMEM] * 5,
        out_specs=(VMEM, VMEM),
        compiler_params=params(32),
        cost_estimate=cost(10**7, 2 * 10**6),
        name="pack_heads",
    )(queries, keys, values, saved_out, out_grad)


def block_terms(tail):
    tail = tail.astype(F32)
    return tail[0:1, :] + tail[1:2, :] + tail[2:3, :]


def score_weights(qg):
    turned = qg.T
    top_half = lax.broadcasted_iota(jnp.int32, turned.shape, 0) < HD
    zero = jnp.zeros_like(turned)
    return jnp.concatenate(
        [jnp.where(top_half, turned, zero), jnp.where(top_half, zero, turned)], axis=1
    )


def grad_weights(qg, factor):
    scaled = (qg.T.astype(F32) * factor).T
    left = lax.broadcasted_iota(jnp.int32, scaled.shape, 1) < HD
    return jnp.concatenate(
        [jnp.where(left, 0.0, scaled), jnp.where(left, scaled, 0.0)], axis=0
    ).astype(BF)


def fold(x, op):
    return op(x.reshape(-1, 8, x.shape[1]), axis=0)


def far_kernel(offs_ref, kv_ref, qg_ref, far_ref, part_ref, stat_ref, near_s, far_s, ed):
    offset = offs_ref[lax.axis_index("inner")]
    qg = qg_ref[offset, :BLOCK, :]
    terms = block_terms(qg_ref[offset, BLOCK:, :])
    weights = score_weights(qg)
    top8 = jnp.full((8, BLOCK), -jnp.inf, F32)
    for c in range(SEG // CHUNK):
        rows = slice(c * CHUNK, (c + 1) * CHUNK)
        blocks = slice(c * CHUNK // BLOCK, (c + 1) * CHUNK // BLOCK)
        near = dot(kv_ref[blocks].reshape(CHUNK, 2 * HD), weights[:, :BLOCK])
        near_s[rows, :] = near
        far = dot(far_ref[blocks].reshape(CHUNK, 2 * HD), weights)
        far_s[rows, :] = far
        top8 = jnp.maximum(top8, jnp.maximum(fold(near, jnp.max), fold(far[:, :BLOCK], jnp.max)))
    top = jnp.max(top8, axis=0, keepdims=True)
    sum8 = jnp.zeros((8, BLOCK), F32)
    for c in range(SEG // CHUNK):
        rows = slice(c * CHUNK, (c + 1) * CHUNK)
        sum8 += fold(jnp.exp(near_s[rows, :] - top), jnp.sum)
        prob = jnp.exp(far_s[rows, :BLOCK] - top)
        sum8 += fold(prob, jnp.sum)
        ed[rows, :BLOCK] = prob.astype(BF)
        ed[rows, BLOCK:] = (prob * (far_s[rows, BLOCK:] - terms)).astype(BF)
    factor = 1.0 / jnp.sum(sum8, axis=0, keepdims=True)
    second = grad_weights(qg, factor)
    query_grad = jnp.zeros((HD, BLOCK), F32)
    for c in range(SEG // CHUNK):
        rows = slice(c * CHUNK, (c + 1) * CHUNK)
        blocks = slice(c * CHUNK // BLOCK, (c + 1) * CHUNK // BLOCK)
        both = ed[rows, :]
        part_ref[blocks] = dot(both, second).astype(BF).reshape(-1, BLOCK, 2 * HD)
        keys = far_ref[blocks].reshape(CHUNK, 2 * HD).T[:HD, :]
        query_grad += dot(keys, both[:, BLOCK:])
    stat_ref[0:1, :] = top
    stat_ref[1:2, :] = factor
    stat_ref[8:, :] = query_grad * factor * (HD**-0.5)


def far_part(offsets, kv, qg, far):
    return pl.pallas_call(
        far_kernel,
        out_shape=(
            jax.ShapeDtypeStruct((NB, BLOCK, 2 * HD), BF),
            jax.ShapeDtypeStruct((8 + HD, BLOCK), F32),
        ),
        in_specs=[SMEM, VMEM, VMEM, VMEM],
        out_specs=(VMEM, VMEM),
        scratch_shapes=[
            pltpu.VMEM((SEG, BLOCK), F32),
            pltpu.VMEM((SEG, 2 * BLOCK), F32),
            pltpu.VMEM((SEG, 2 * BLOCK), BF),
        ],
        compiler_params=params(32),
        cost_estimate=cost(2 * 10**9, 2 * 10**6),
        name="far_part",
    )(offsets, kv, qg, far)


def near_kernel(
    offs_ref, kv_ref, qg_ref, stat_ref, out_ref, pick_ref, keys_t, s0, s1, e0, e1, acc, st0, st1
):
    offset = offs_ref[lax.axis_index("inner")]
    score_refs, grad_refs, stats = (s0, s1), (e0, e1), (st0, st1)
    acc[...] = jnp.zeros_like(acc)
    for b in range(NB):
        keys_t[:, b * BLOCK : (b + 1) * BLOCK] = kv_ref[b].T[:HD, :]

    def step(j, slot, first, second, third):
        s_now, s_old = score_refs[slot], score_refs[1 - slot]
        e_now, e_old = grad_refs[1 - slot], grad_refs[slot]
        st_now, st_old = stats[slot], stats[1 - slot]
        if first:
            weights = score_weights(qg_ref[j, :BLOCK, :])
            top8 = jnp.full((8, BLOCK), -jnp.inf, F32)
        if second:
            picked1 = (j - 1) == offset
            terms = block_terms(qg_ref[j - 1, BLOCK:, :])
            top = st_old[0:1, :]
            sum8 = jnp.zeros((8, BLOCK), F32)
        if third:
            picked2 = (j - 2) == offset
            factor = st_now[1:2, :]
            gweights = grad_weights(qg_ref[j - 2, :BLOCK, :], factor)
            query_grad = jnp.zeros((HD, BLOCK), F32)
        for c in range(SEG // CHUNK):
            rows = slice(c * CHUNK, (c + 1) * CHUNK)
            blocks = slice(c * CHUNK // BLOCK, (c + 1) * CHUNK // BLOCK)
            if third:
                both = e_old[rows, :]
                acc[rows, :] += dot(both, gweights)
                query_grad += dot(keys_t[:, rows], both[:, BLOCK:])
            if first:
                score = dot(kv_ref[blocks].reshape(CHUNK, 2 * HD), weights)
                s_now[rows, :] = score
                top8 = jnp.maximum(top8, fold(score[:, :BLOCK], jnp.max))
            if second:
                prob = jnp.exp(s_old[rows, :BLOCK] - top)
                sum8 += fold(prob, jnp.sum)
                e_now[rows, :BLOCK] = prob.astype(BF)
                e_now[rows, BLOCK:] = (prob * (s_old[rows, BLOCK:] - terms)).astype(BF)
        if third:
            query_grad = query_grad * (factor * (HD**-0.5))
            query_grad += jnp.where(picked2, stat_ref[8:, :], 0.0)
            out_ref[j - 2, BLOCK:, :] = query_grad.astype(BF)
        if first:
            top = jnp.max(top8, axis=0, keepdims=True)
            st_now[0:1, :] = jnp.where(j == offset, stat_ref[0:1, :], top)
        if second:
            total = jnp.sum(sum8, axis=0, keepdims=True)
            st_old[1:2, :] = jnp.where(picked1, stat_ref[1:2, :], 1.0 / total)

    step(0, 0, True, False, False)
    step(1, 1, True, True, False)

    def pair(i, carry):
        step(2 * i, 0, True, True, True)
        step(2 * i + 1, 1, True, True, True)
        return carry

    lax.fori_loop(1, NB // 2, pair, 0)
    step(NB, 0, False, True, True)
    step(NB + 1, 1, False, False, True)
    for b in range(NB):
        out_ref[b, :BLOCK, :] = acc[b * BLOCK : (b + 1) * BLOCK, :].astype(BF)
    pick_ref[...] = acc[pl.ds(pl.multiple_of(offset * BLOCK, BLOCK), BLOCK), :]


def near_part(offsets, kv, qg, stat):
    return pl.pallas_call(
        near_kernel,
        out_shape=(
            jax.ShapeDtypeStruct((NB, OUT_ROWS, BLOCK), BF),
            jax.ShapeDtypeStruct((BLOCK, 2 * HD), F32),
        ),
        in_specs=[SMEM, VMEM, VMEM, VMEM],
        out_specs=(VMEM, VMEM),
        scratch_shapes=[
            pltpu.VMEM((HD, SEG), BF),
            pltpu.VMEM((SEG, 2 * BLOCK), F32),
            pltpu.VMEM((SEG, 2 * BLOCK), F32),
            pltpu.VMEM((SEG, 2 * BLOCK), BF),
            pltpu.VMEM((SEG, 2 * BLOCK), BF),
            pltpu.VMEM((SEG, 2 * HD), F32),
            pltpu.VMEM((8, BLOCK), F32),
            pltpu.VMEM((8, BLOCK), F32),
        ],
        compiler_params=params(40),
        cost_estimate=cost(15 * 10**9, 4 * 10**6, SEG * SEG),
        name="near_part",
    )(offsets, kv, qg, stat)


def finish_kernel(offs_ref, pick_ref, parts_ref, whole_ref, out_ref):
    del offs_ref, whole_ref
    total = pick_ref[...]
    for n in range(NB):
        total += parts_ref[n].astype(F32)
    out_ref[0] = total.astype(BF)


def finish(head_offset, pick, parts, whole):
    return pl.pallas_call(
        finish_kernel,
        out_shape=jax.ShapeDtypeStruct((NB, OUT_ROWS, BLOCK), BF),
        grid_spec=pltpu.PrefetchScalarGridSpec(
            num_scalar_prefetch=1,
            grid=(1,),
            in_specs=[
                pl.BlockSpec((BLOCK, 2 * HD), lambda i, off: (0, 0)),
                pl.BlockSpec((NB, BLOCK, 2 * HD), lambda i, off: (0, 0, 0)),
                pl.BlockSpec(memory_space=pl.ANY),
            ],
            out_specs=pl.BlockSpec((1, BLOCK, 2 * HD), lambda i, off: (off[0], 0, 0)),
        ),
        input_output_aliases={3: 0},
        cost_estimate=cost(10**6, 10**6),
        name="finish_picked",
    )(head_offset, pick, parts, whole)


def unpack_kernel(in_ref, q_ref, k_ref, v_ref):
    for pair in range(HEADS // 2):
        cols = slice(pair * 2 * HD, (pair + 1) * 2 * HD)
        one, two = in_ref[2 * pair, :BLOCK, :], in_ref[2 * pair + 1, :BLOCK, :]
        k_ref[:, cols] = jnp.concatenate([one[:, :HD], two[:, :HD]], axis=1)
        v_ref[:, cols] = jnp.concatenate([one[:, HD:], two[:, HD:]], axis=1)
        turned = jnp.concatenate(
            [in_ref[2 * pair, BLOCK:, :], in_ref[2 * pair + 1, BLOCK:, :]], axis=0
        )
        q_ref[:, cols] = turned.T


def unpack(block):
    shape = jax.ShapeDtypeStruct((BLOCK, HEADS * HD), BF)
    return pl.pallas_call(
        unpack_kernel,
        out_shape=(shape, shape, shape),
        in_specs=[VMEM],
        out_specs=(VMEM, VMEM, VMEM),
        compiler_params=params(32),
        cost_estimate=cost(10**6, 2 * 10**6),
        name="unpack_heads",
    )(block)


def exchange(array, axis):
    return lax.all_to_all(array, axis, split_axis=0, concat_axis=0, tiled=True)


def on_device(queries, keys, values, saved_out, out_grad, offsets):
    head_offset = lax.dynamic_slice_in_dim(offsets, lax.axis_index("inner"), 1)
    kv, qg = pack(queries, keys, values, saved_out, out_grad)
    kv = exchange(kv, "inner")
    picked = lax.dynamic_index_in_dim(kv, head_offset[0], 0, keepdims=True)
    far = exchange(jnp.broadcast_to(picked, kv.shape), "outer")
    qg = exchange(qg, "inner")
    parts, stat = far_part(offsets, kv, qg, far)
    parts = exchange(parts, "outer")
    whole, pick = near_part(offsets, kv, qg, stat)
    whole = finish(head_offset, pick, parts, whole)
    return unpack(exchange(whole, "inner"))


def solution(mesh):
    rows = P(("outer", "inner"), None)
    return jax.shard_map(
        on_device,
        mesh=mesh,
        in_specs=(rows, rows, rows, rows, rows, P()),
        out_specs=(rows, rows, rows),
        check_vma=False,
    )
```

```python
import jax
import jax.numpy as jnp
from jax import lax
from jax.experimental import pallas as pl
from jax.experimental.pallas import tpu as pltpu
from jax.sharding import PartitionSpec as P

HEADS = 16
HD = 64
BLOCK = 128
NB = 16
RING = 4
SEG = NB * BLOCK
CHUNK = 256
BF = jnp.bfloat16
F32 = jnp.float32
VMEM = pl.BlockSpec(memory_space=pltpu.VMEM)
SMEM = pl.BlockSpec(memory_space=pltpu.SMEM)
QG_ROWS = BLOCK + 16
OUT_ROWS = BLOCK + HD


def params(mib):
    return pltpu.CompilerParams(vmem_limit_bytes=mib * 1024 * 1024)


def cost(flops, nbytes, exps=0):
    return pl.CostEstimate(flops=flops, bytes_accessed=nbytes, transcendentals=exps)


def dot(a, b):
    return jnp.dot(a, b, preferred_element_type=F32)


def dot_nt(a, b):
    return lax.dot_general(a, b, (((1,), (1,)), ((), ())), preferred_element_type=F32)


def split3(x):
    high = x.astype(BF)
    rest = x - high.astype(F32)
    mid = rest.astype(BF)
    low = (rest - mid.astype(F32)).astype(BF)
    return high, mid, low


def pack_kernel(q_in, k_in, v_in, o_in, g_in, kv_ref, qg_ref, q_ref, k_ref, v_ref, o_ref, g_ref, sems):
    copies = [
        pltpu.make_async_copy(source, target, sems.at[n])
        for n, (source, target) in enumerate(
            ((g_in, g_ref), (o_in, o_ref), (q_in, q_ref), (k_in, k_ref), (v_in, v_ref))
        )
    ]
    for copy in copies:
        copy.start()
    copies[0].wait()
    copies[1].wait()
    head_of = lax.broadcasted_iota(jnp.int32, (HEADS, HEADS * HD), 1) // HD
    mine = head_of == lax.broadcasted_iota(jnp.int32, (HEADS, HEADS * HD), 0)
    ones = jnp.where(mine, 1.0, 0.0).astype(BF)
    product = g_ref[...].astype(F32) * o_ref[...].astype(F32)
    high = product.astype(BF)
    low = (product - high.astype(F32)).astype(BF)
    terms = dot_nt(ones, high) + dot_nt(ones, low)
    parts = [part.astype(F32) for part in split3(terms)]
    row = lax.broadcasted_iota(jnp.int32, (16, BLOCK), 0)
    for copy in copies[2:]:
        copy.wait()
    for pair in range(HEADS // 2):
        cols = slice(pair * 2 * HD, (pair + 1) * 2 * HD)
        q, k, v, g = (
            (q_ref[:, cols].astype(F32) * (HD**-0.5)).astype(BF),
            k_ref[:, cols],
            v_ref[:, cols],
            g_ref[:, cols],
        )
        for sub in range(2):
            head = 2 * pair + sub
            half = slice(sub * HD, (sub + 1) * HD)
            kv_ref[head] = jnp.concatenate([k[:, half], v[:, half]], axis=1)
            qg_ref[head, :BLOCK, :] = jnp.concatenate([q[:, half], g[:, half]], axis=1)
            tail = jnp.zeros((16, BLOCK), F32)
            for n, part in enumerate(parts):
                tail = jnp.where(row == n, part[head : head + 1, :], tail)
            qg_ref[head, BLOCK:, :] = tail.astype(BF)


def pack(queries, keys, values, saved_out, out_grad):
    return pl.pallas_call(
        pack_kernel,
        out_shape=(
            jax.ShapeDtypeStruct((HEADS, BLOCK, 2 * HD), BF),
            jax.ShapeDtypeStruct((HEADS, QG_ROWS, 2 * HD), BF),
        ),
        in_specs=[pl.BlockSpec(memory_space=pl.ANY)] * 5,
        out_specs=(VMEM, VMEM),
        scratch_shapes=[pltpu.VMEM((BLOCK, HEADS * HD), BF)] * 5 + [pltpu.SemaphoreType.DMA((5,))],
        compiler_params=params(60),
        cost_estimate=cost(10**7, 2 * 10**6),
        name="pack_heads",
    )(queries, keys, values, saved_out, out_grad)


def pick_kernel(offs_ref, kv_ref, out_ref):
    out_ref[...] = kv_ref[offs_ref[lax.axis_index("inner")]]


def pick(offsets, kv):
    return pl.pallas_call(
        pick_kernel,
        out_shape=jax.ShapeDtypeStruct(kv.shape[1:], kv.dtype),
        in_specs=[SMEM, VMEM],
        out_specs=VMEM,
        compiler_params=params(16),
        cost_estimate=cost(10**3, 10**5),
        name="pick_block",
    )(offsets, kv)


def block_terms(tail):
    tail = tail.astype(F32)
    return tail[0:1, :] + tail[1:2, :] + tail[2:3, :]


def score_weights(qg):
    turned = qg.T
    top_half = lax.broadcasted_iota(jnp.int32, turned.shape, 0) < HD
    zero = jnp.zeros_like(turned)
    return jnp.concatenate(
        [jnp.where(top_half, turned, zero), jnp.where(top_half, zero, turned)], axis=1
    )


def grad_weights(qg, factor):
    scaled = (qg.T.astype(F32) * factor).T
    left = lax.broadcasted_iota(jnp.int32, scaled.shape, 1) < HD
    return jnp.concatenate(
        [jnp.where(left, 0.0, scaled), jnp.where(left, scaled, 0.0)], axis=0
    ).astype(BF)


def fold(x, op):
    return op(x.reshape(-1, 8, x.shape[1]), axis=0)


def far_kernel(
    offs_ref, kv_ref, qg_ref, far0, far1, far2, far3, part_ref, stat_ref, near_s, far_s, ed
):
    offset = offs_ref[lax.axis_index("inner")]
    place = lax.axis_index("outer")
    place_x, place_y = place // RING, place % RING
    fars = (far0, far1, far2, far3)

    def far_rows(c):
        per = CHUNK // BLOCK
        a, b = divmod(c * per, RING)
        return fars[a][b : b + per].reshape(CHUNK, 2 * HD)

    qg = qg_ref[offset, :BLOCK, :]
    terms = block_terms(qg_ref[offset, BLOCK:, :])
    weights = score_weights(qg)
    top8 = jnp.full((8, BLOCK), -jnp.inf, F32)
    for c in range(SEG // CHUNK):
        rows = slice(c * CHUNK, (c + 1) * CHUNK)
        blocks = slice(c * CHUNK // BLOCK, (c + 1) * CHUNK // BLOCK)
        near = dot(kv_ref[blocks].reshape(CHUNK, 2 * HD), weights[:, :BLOCK])
        near_s[rows, :] = near
        far = dot(far_rows(c), weights)
        far_s[rows, :] = far
        top8 = jnp.maximum(top8, jnp.maximum(fold(near, jnp.max), fold(far[:, :BLOCK], jnp.max)))
    top = jnp.max(top8, axis=0, keepdims=True)
    sum8 = jnp.zeros((8, BLOCK), F32)
    for c in range(SEG // CHUNK):
        rows = slice(c * CHUNK, (c + 1) * CHUNK)
        sum8 += fold(jnp.exp(near_s[rows, :] - top), jnp.sum)
        prob = jnp.exp(far_s[rows, :BLOCK] - top)
        sum8 += fold(prob, jnp.sum)
        ed[rows, :BLOCK] = prob.astype(BF)
        ed[rows, BLOCK:] = (prob * (far_s[rows, BLOCK:] - terms)).astype(BF)
    factor = 1.0 / jnp.sum(sum8, axis=0, keepdims=True)
    second = grad_weights(qg, factor)
    query_grad = jnp.zeros((HD, BLOCK), F32)
    for c in range(SEG // CHUNK):
        rows = slice(c * CHUNK, (c + 1) * CHUNK)
        both = ed[rows, :]
        grads = dot(both, second).astype(BF)
        for n in range(CHUNK // BLOCK):
            a, b = divmod(c * CHUNK // BLOCK + n, RING)
            owner = (place_x + a) % RING * RING + (place_y + b) % RING
            part_ref[owner] = grads[n * BLOCK : (n + 1) * BLOCK, :]
        keys = far_rows(c).T[:HD, :]
        query_grad += dot(keys, both[:, BLOCK:])
    stat_ref[0:1, :] = top
    stat_ref[1:2, :] = factor
    stat_ref[8:, :] = query_grad * factor * (HD**-0.5)


def far_part(offsets, kv, qg, fars):
    return pl.pallas_call(
        far_kernel,
        out_shape=(
            jax.ShapeDtypeStruct((NB, BLOCK, 2 * HD), BF),
            jax.ShapeDtypeStruct((8 + HD, BLOCK), F32),
        ),
        in_specs=[SMEM] + [VMEM] * 6,
        out_specs=(VMEM, VMEM),
        scratch_shapes=[
            pltpu.VMEM((SEG, BLOCK), F32),
            pltpu.VMEM((SEG, 2 * BLOCK), F32),
            pltpu.VMEM((SEG, 2 * BLOCK), BF),
        ],
        compiler_params=params(32),
        cost_estimate=cost(2 * 10**9, 2 * 10**6),
        name="far_part",
    )(offsets, kv, qg, *fars)


def near_kernel(
    offs_ref, kv_ref, qg_ref, stat_ref, dq_ref, acc, keys_t, s0, s1, e0, e1, st0, st1
):
    offset = offs_ref[lax.axis_index("inner")]
    score_refs, grad_refs, stats = (s0, s1), (e0, e1), (st0, st1)
    acc[...] = jnp.zeros_like(acc)
    for b in range(NB):
        keys_t[:, b * BLOCK : (b + 1) * BLOCK] = kv_ref[b].T[:HD, :]

    def step(j, slot, first, second, third):
        s_now, s_old = score_refs[slot], score_refs[1 - slot]
        e_now, e_old = grad_refs[1 - slot], grad_refs[slot]
        st_now, st_old = stats[slot], stats[1 - slot]
        if first:
            weights = score_weights(qg_ref[j, :BLOCK, :])
            top8 = jnp.full((8, BLOCK), -jnp.inf, F32)
        if second:
            picked1 = (j - 1) == offset
            terms = block_terms(qg_ref[j - 1, BLOCK:, :])
            top = st_old[0:1, :]
            sum8 = jnp.zeros((8, BLOCK), F32)
        if third:
            picked2 = (j - 2) == offset
            factor = st_now[1:2, :]
            gweights = grad_weights(qg_ref[j - 2, :BLOCK, :], factor)
            query_grad = jnp.zeros((HD, BLOCK), F32)
        for c in range(SEG // CHUNK):
            rows = slice(c * CHUNK, (c + 1) * CHUNK)
            blocks = slice(c * CHUNK // BLOCK, (c + 1) * CHUNK // BLOCK)
            if third:
                both = e_old[rows, :]
                acc[rows, :] += dot(both, gweights)
                query_grad += dot(keys_t[:, rows], both[:, BLOCK:])
            if first:
                score = dot(kv_ref[blocks].reshape(CHUNK, 2 * HD), weights)
                s_now[rows, :] = score
                top8 = jnp.maximum(top8, fold(score[:, :BLOCK], jnp.max))
            if second:
                prob = jnp.exp(s_old[rows, :BLOCK] - top)
                sum8 += fold(prob, jnp.sum)
                e_now[rows, :BLOCK] = prob.astype(BF)
                e_now[rows, BLOCK:] = (prob * (s_old[rows, BLOCK:] - terms)).astype(BF)
        if third:
            query_grad = query_grad * (factor * (HD**-0.5))
            query_grad += jnp.where(picked2, stat_ref[8:, :], 0.0)
            dq_ref[j - 2] = query_grad.astype(BF)
        if first:
            top = jnp.max(top8, axis=0, keepdims=True)
            st_now[0:1, :] = jnp.where(j == offset, stat_ref[0:1, :], top)
        if second:
            total = jnp.sum(sum8, axis=0, keepdims=True)
            st_old[1:2, :] = jnp.where(picked1, stat_ref[1:2, :], 1.0 / total)

    step(0, 0, True, False, False)
    step(1, 1, True, True, False)

    def pair(i, carry):
        step(2 * i, 0, True, True, True)
        step(2 * i + 1, 1, True, True, True)
        return carry

    lax.fori_loop(1, NB // 2, pair, 0)
    step(NB, 0, False, True, True)
    step(NB + 1, 1, False, False, True)


def near_part(offsets, kv, qg, stat):
    return pl.pallas_call(
        near_kernel,
        out_shape=(
            jax.ShapeDtypeStruct((NB, HD, BLOCK), BF),
            jax.ShapeDtypeStruct((SEG, 2 * HD), F32),
        ),
        in_specs=[SMEM, VMEM, VMEM, VMEM],
        out_specs=(VMEM, VMEM),
        scratch_shapes=[
            pltpu.VMEM((HD, SEG), BF),
            pltpu.VMEM((SEG, 2 * BLOCK), F32),
            pltpu.VMEM((SEG, 2 * BLOCK), F32),
            pltpu.VMEM((SEG, 2 * BLOCK), BF),
            pltpu.VMEM((SEG, 2 * BLOCK), BF),
            pltpu.VMEM((8, BLOCK), F32),
            pltpu.VMEM((8, BLOCK), F32),
        ],
        compiler_params=params(40),
        cost_estimate=cost(15 * 10**9, 4 * 10**6, SEG * SEG),
        name="near_part",
    )(offsets, kv, qg, stat)


def finish_kernel(offs_ref, dq_ref, acc, parts_ref, out_ref):
    offset = offs_ref[lax.axis_index("inner")]
    for b in range(NB):
        out_ref[b, :BLOCK, :] = acc[b * BLOCK : (b + 1) * BLOCK, :].astype(BF)
        out_ref[b, BLOCK:, :] = dq_ref[b]
    total = acc[pl.ds(pl.multiple_of(offset * BLOCK, BLOCK), BLOCK), :]
    for n in range(NB):
        total += parts_ref[n].astype(F32)
    out_ref[offset, :BLOCK, :] = total.astype(BF)


def finish(offsets, dq, sums, parts):
    return pl.pallas_call(
        finish_kernel,
        out_shape=jax.ShapeDtypeStruct((NB, OUT_ROWS, BLOCK), BF),
        in_specs=[SMEM, VMEM, VMEM, VMEM],
        out_specs=VMEM,
        compiler_params=params(32),
        cost_estimate=cost(10**6, 10**6),
        name="finish_picked",
    )(offsets, dq, sums, parts)


def unpack_kernel(in_ref, q_ref, k_ref, v_ref):
    for pair in range(HEADS // 2):
        cols = slice(pair * 2 * HD, (pair + 1) * 2 * HD)
        one, two = in_ref[2 * pair, :BLOCK, :], in_ref[2 * pair + 1, :BLOCK, :]
        k_ref[:, cols] = jnp.concatenate([one[:, :HD], two[:, :HD]], axis=1)
        v_ref[:, cols] = jnp.concatenate([one[:, HD:], two[:, HD:]], axis=1)
        turned = jnp.concatenate(
            [in_ref[2 * pair, BLOCK:, :], in_ref[2 * pair + 1, BLOCK:, :]], axis=0
        )
        q_ref[:, cols] = turned.T


def unpack(block):
    shape = jax.ShapeDtypeStruct((BLOCK, HEADS * HD), BF)
    return pl.pallas_call(
        unpack_kernel,
        out_shape=(shape, shape, shape),
        in_specs=[VMEM],
        out_specs=(VMEM, VMEM, VMEM),
        compiler_params=params(32),
        cost_estimate=cost(10**6, 2 * 10**6),
        name="unpack_heads",
    )(block)


def exchange(array, axis):
    return lax.all_to_all(array, axis, split_axis=0, concat_axis=0, tiled=True)


def spread(block):
    def ring(step, along_x):
        pairs = []
        for x in range(RING):
            for y in range(RING):
                source = (x + step) % RING * RING + y if along_x else x * RING + (y + step) % RING
                pairs.append((source, x * RING + y))
        return pairs

    row = jnp.stack([block] + [lax.ppermute(block, "outer", ring(n, False)) for n in (1, 2, 3)])
    return [row] + [lax.ppermute(row, "outer", ring(n, True)) for n in (1, 2, 3)]


def on_device(queries, keys, values, saved_out, out_grad, offsets):
    kv, qg = pack(queries, keys, values, saved_out, out_grad)
    kv = exchange(kv, "inner")
    fars = spread(pick(offsets, kv))
    qg = exchange(qg, "inner")
    parts, stat = far_part(offsets, kv, qg, fars)
    parts = exchange(parts, "outer")
    dq, sums = near_part(offsets, kv, qg, stat)
    whole = finish(offsets, dq, sums, parts)
    return unpack(exchange(whole, "inner"))


def solution(mesh):
    rows = P(("outer", "inner"), None)
    return jax.shard_map(
        on_device,
        mesh=mesh,
        in_specs=(rows, rows, rows, rows, rows, P()),
        out_specs=(rows, rows, rows),
        check_vma=False,
    )
```

```python
import jax
import jax.numpy as jnp
from jax import lax
from jax.experimental import pallas as pl
from jax.experimental.pallas import tpu as pltpu
from jax.sharding import PartitionSpec as P

HEADS = 16
HD = 64
BLOCK = 128
NB = 16
RING = 4
GROUP = 4
GROUPS = HEADS // GROUP
GROUP_COLS = GROUP * HD
SEG = NB * BLOCK
CHUNK = 256
BF = jnp.bfloat16
F32 = jnp.float32
VMEM = pl.BlockSpec(memory_space=pltpu.VMEM)
SMEM = pl.BlockSpec(memory_space=pltpu.SMEM)
QG_ROWS = BLOCK + 16
OUT_ROWS = BLOCK + HD


def params(mib):
    return pltpu.CompilerParams(vmem_limit_bytes=mib * 1024 * 1024)


def cost(flops, nbytes, exps=0):
    return pl.CostEstimate(flops=flops, bytes_accessed=nbytes, transcendentals=exps)


def dot(a, b):
    return jnp.dot(a, b, preferred_element_type=F32)


def dot_nt(a, b):
    return lax.dot_general(a, b, (((1,), (1,)), ((), ())), preferred_element_type=F32)


def split3(x):
    high = x.astype(BF)
    rest = x - high.astype(F32)
    mid = rest.astype(BF)
    low = (rest - mid.astype(F32)).astype(BF)
    return high, mid, low


ANY = pl.BlockSpec(memory_space=pl.ANY)


def fetch(pairs, sems):
    copies = [
        pltpu.make_async_copy(source, target, sems.at[n]) for n, (source, target) in enumerate(pairs)
    ]
    for copy in copies:
        copy.start()
    return copies


def half_of(ref, head):
    start = head * HD
    return ref[:, start : start + HD]


def pack_kv_kernel(k_in, v_in, kv_out, k_ref, v_ref, kv_ref, sems, out_sems):
    copies = []
    for n in range(GROUPS):
        cols = pl.ds(n * GROUP_COLS, GROUP_COLS)
        pairs = ((k_in.at[:, cols], k_ref.at[:, cols]), (v_in.at[:, cols], v_ref.at[:, cols]))
        copies.append(fetch(pairs, sems.at[n]))
    outs = []
    for n in range(GROUPS):
        for copy in copies[n]:
            copy.wait()
        for head in range(n * GROUP, (n + 1) * GROUP):
            kv_ref[head] = jnp.concatenate([half_of(k_ref, head), half_of(v_ref, head)], axis=1)
        heads = pl.ds(n * GROUP, GROUP)
        outs.append(pltpu.make_async_copy(kv_ref.at[heads], kv_out.at[heads], out_sems.at[n]))
        outs[n].start()
    for out in outs:
        out.wait()


def pack_kv(keys, values):
    return pl.pallas_call(
        pack_kv_kernel,
        out_shape=jax.ShapeDtypeStruct((HEADS, BLOCK, 2 * HD), BF),
        in_specs=[ANY] * 2,
        out_specs=ANY,
        scratch_shapes=[pltpu.VMEM((BLOCK, HEADS * HD), BF)] * 2
        + [
            pltpu.VMEM((HEADS, BLOCK, 2 * HD), BF),
            pltpu.SemaphoreType.DMA((GROUPS, 2)),
            pltpu.SemaphoreType.DMA((GROUPS,)),
        ],
        compiler_params=params(60),
        cost_estimate=cost(10**6, 10**6),
        name="pack_keys_values",
    )(keys, values)


def pack_qg_kernel(q_in, o_in, g_in, qg_ref, q_ref, o_ref, g_ref, sems):
    copies = fetch(((g_in, g_ref), (o_in, o_ref), (q_in, q_ref)), sems)
    copies[0].wait()
    copies[1].wait()
    head_of = lax.broadcasted_iota(jnp.int32, (HEADS, HEADS * HD), 1) // HD
    mine = head_of == lax.broadcasted_iota(jnp.int32, (HEADS, HEADS * HD), 0)
    ones = jnp.where(mine, 1.0, 0.0).astype(BF)
    product = g_ref[...].astype(F32) * o_ref[...].astype(F32)
    high = product.astype(BF)
    low = (product - high.astype(F32)).astype(BF)
    terms = dot_nt(ones, high) + dot_nt(ones, low)
    parts = [part.astype(F32) for part in split3(terms)]
    row = lax.broadcasted_iota(jnp.int32, (16, BLOCK), 0)
    copies[2].wait()
    for head in range(HEADS):
        q = (half_of(q_ref, head).astype(F32) * (HD**-0.5)).astype(BF)
        qg_ref[head, :BLOCK, :] = jnp.concatenate([q, half_of(g_ref, head)], axis=1)
        tail = jnp.zeros((16, BLOCK), F32)
        for n, part in enumerate(parts):
            tail = jnp.where(row == n, part[head : head + 1, :], tail)
        qg_ref[head, BLOCK:, :] = tail.astype(BF)


def pack_qg(queries, saved_out, out_grad):
    return pl.pallas_call(
        pack_qg_kernel,
        out_shape=jax.ShapeDtypeStruct((HEADS, QG_ROWS, 2 * HD), BF),
        in_specs=[ANY] * 3,
        out_specs=VMEM,
        scratch_shapes=[pltpu.VMEM((BLOCK, HEADS * HD), BF)] * 3 + [pltpu.SemaphoreType.DMA((3,))],
        compiler_params=params(60),
        cost_estimate=cost(10**7, 2 * 10**6),
        name="pack_queries_grads",
    )(queries, saved_out, out_grad)


def pick_kernel(offs_ref, kv_ref, out_ref):
    out_ref[...] = kv_ref[offs_ref[lax.axis_index("inner")]]


def pick(offsets, kv):
    return pl.pallas_call(
        pick_kernel,
        out_shape=jax.ShapeDtypeStruct(kv.shape[1:], kv.dtype),
        in_specs=[SMEM, VMEM],
        out_specs=VMEM,
        compiler_params=params(4),
        cost_estimate=cost(10**3, 10**5),
        name="pick_block",
    )(offsets, kv)


def block_terms(tail):
    tail = tail.astype(F32)
    return tail[0:1, :] + tail[1:2, :] + tail[2:3, :]


def score_weights(q_turned, g_turned):
    zero = jnp.zeros((HD, BLOCK), BF)
    none = zero if q_turned is None else q_turned
    grad = zero if g_turned is None else g_turned
    return jnp.concatenate(
        [jnp.concatenate([none, zero], axis=1), jnp.concatenate([zero, grad], axis=1)], axis=0
    )


def grad_weights(turned, factor):
    scaled = (turned.astype(F32) * factor).T.astype(BF)
    left = lax.broadcasted_iota(jnp.int32, scaled.shape, 1) < HD
    zero = jnp.zeros_like(scaled)
    return jnp.concatenate(
        [jnp.where(left, zero, scaled), jnp.where(left, scaled, zero)], axis=0
    )


def kv_rows(kv_ref, c):
    per = CHUNK // BLOCK
    return kv_ref[c * per : (c + 1) * per].reshape(CHUNK, 2 * HD)


def fold(x, op):
    return op(x.reshape(-1, 8, x.shape[1]), axis=0)


def prepare_kernel(offs_ref, kv_ref, qg_ref, stat_ref, near_s):
    offset = offs_ref[lax.axis_index("inner")]
    weights = qg_ref[offset, :BLOCK, :].T
    top_half = lax.broadcasted_iota(jnp.int32, weights.shape, 0) < HD
    weights = jnp.where(top_half, weights, jnp.zeros_like(weights))
    top8 = jnp.full((8, BLOCK), -jnp.inf, F32)
    for c in range(SEG // CHUNK):
        near = dot(kv_rows(kv_ref, c), weights)
        near_s[c * CHUNK : (c + 1) * CHUNK, :] = near
        top8 = jnp.maximum(top8, fold(near, jnp.max))
    top = jnp.max(top8, axis=0, keepdims=True)
    sum8 = jnp.zeros((8, BLOCK), F32)
    for c in range(SEG // CHUNK):
        sum8 += fold(jnp.exp(near_s[c * CHUNK : (c + 1) * CHUNK, :] - top), jnp.sum)
    stat_ref[0:1, :] = top
    stat_ref[1:2, :] = jnp.sum(sum8, axis=0, keepdims=True)


def prepare(offsets, kv, qg):
    return pl.pallas_call(
        prepare_kernel,
        out_shape=jax.ShapeDtypeStruct((8, BLOCK), F32),
        in_specs=[SMEM, VMEM, VMEM],
        out_specs=VMEM,
        scratch_shapes=[pltpu.VMEM((SEG, BLOCK), F32)],
        compiler_params=params(20),
        cost_estimate=cost(10**9, 2 * 10**6),
        name="prepare_near",
    )(offsets, kv, qg)


def far_kernel(
    offs_ref, qg_ref, near_ref, far0, far1, far2, far3, part_ref, stat_ref, far_s, ed
):
    offset = offs_ref[lax.axis_index("inner")]
    place = lax.axis_index("outer")
    place_x, place_y = place // RING, place % RING
    fars = (far0, far1, far2, far3)

    def far_rows(c):
        per = CHUNK // BLOCK
        a, b = divmod(c * per, RING)
        return fars[a][b : b + per].reshape(CHUNK, 2 * HD)

    terms = block_terms(qg_ref[offset, BLOCK:, :])
    turned = qg_ref[offset, :BLOCK, :].T
    weights = score_weights(turned[:HD, :], turned[HD:, :])
    near_top = near_ref[0:1, :]
    top8 = jnp.broadcast_to(near_top, (8, BLOCK))
    for c in range(SEG // CHUNK):
        rows = slice(c * CHUNK, (c + 1) * CHUNK)
        far = dot(far_rows(c), weights)
        far_s[rows, :] = far
        top8 = jnp.maximum(top8, fold(far[:, :BLOCK], jnp.max))
    top = jnp.max(top8, axis=0, keepdims=True)
    sum8 = jnp.zeros((8, BLOCK), F32)
    for c in range(SEG // CHUNK):
        rows = slice(c * CHUNK, (c + 1) * CHUNK)
        prob = jnp.exp(far_s[rows, :BLOCK] - top)
        sum8 += fold(prob, jnp.sum)
        ed[rows, :BLOCK] = prob.astype(BF)
        ed[rows, BLOCK:] = (prob * (far_s[rows, BLOCK:] - terms)).astype(BF)
    total = jnp.sum(sum8, axis=0, keepdims=True) + near_ref[1:2, :] * jnp.exp(near_top - top)
    factor = 1.0 / total
    second = grad_weights(turned, factor)
    query_grad = jnp.zeros((HD, BLOCK), F32)
    for c in range(SEG // CHUNK):
        rows = slice(c * CHUNK, (c + 1) * CHUNK)
        both = ed[rows, :]
        grads = dot(both, second).astype(BF)
        for n in range(CHUNK // BLOCK):
            a, b = divmod(c * CHUNK // BLOCK + n, RING)
            owner = (place_x + a) % RING * RING + (place_y + b) % RING
            part_ref[owner] = grads[n * BLOCK : (n + 1) * BLOCK, :]
        query_grad += dot(far_rows(c).T[:HD, :], both[:, BLOCK:])
    stat_ref[0:1, :] = top
    stat_ref[1:2, :] = factor
    stat_ref[8:, :] = query_grad * factor * (HD**-0.5)


def far_part(offsets, qg, near_stat, fars):
    return pl.pallas_call(
        far_kernel,
        out_shape=(
            jax.ShapeDtypeStruct((NB, BLOCK, 2 * HD), BF),
            jax.ShapeDtypeStruct((8 + HD, BLOCK), F32),
        ),
        in_specs=[SMEM] + [VMEM] * 6,
        out_specs=(VMEM, VMEM),
        scratch_shapes=[
            pltpu.VMEM((SEG, 2 * BLOCK), F32),
            pltpu.VMEM((SEG, 2 * BLOCK), BF),
        ],
        compiler_params=params(20),
        cost_estimate=cost(2 * 10**9, 2 * 10**6),
        name="far_part",
    )(offsets, qg, near_stat, *fars)


def near_kernel(
    offs_ref, kv_ref, qg_ref, stat_ref, dq_ref, acc, keys_t, turned_ref, s0, s1, e0, e1, st0, st1
):
    offset = offs_ref[lax.axis_index("inner")]
    score_refs, grad_refs, stats = (s0, s1), (e0, e1), (st0, st1)
    chunks = SEG // CHUNK
    for b in range(NB):
        keys_t[:, b * BLOCK : (b + 1) * BLOCK] = kv_ref[b].T[:HD, :]
        turned_ref[b] = qg_ref[b, :BLOCK, :].T

    def step(j, slot, first, second, third):
        s_now, s_old = score_refs[slot], score_refs[1 - slot]
        e_now, e_old = grad_refs[1 - slot], grad_refs[slot]
        st_now, st_old = stats[slot], stats[1 - slot]
        top8 = jnp.full((8, BLOCK), -jnp.inf, F32)
        sum8 = jnp.zeros((8, BLOCK), F32)
        query_grad = jnp.zeros((HD, BLOCK), F32)
        if first or second:
            weights = score_weights(
                turned_ref[j, :HD, :] if first else None,
                turned_ref[j - 1, HD:, :] if second else None,
            )
        if second:
            terms = block_terms(qg_ref[j - 1, BLOCK:, :])
            top = st_old[0:1, :]
        if third:
            factor = st_now[1:2, :]
            gweights = grad_weights(turned_ref[j - 2], factor)
        for c in range(chunks + 1):
            if c < chunks and (first or second):
                rows = slice(c * CHUNK, (c + 1) * CHUNK)
                score = dot(kv_rows(kv_ref, c), weights)
                if first:
                    s_now[rows, :] = score[:, :BLOCK]
                    top8 = jnp.maximum(top8, fold(score[:, :BLOCK], jnp.max))
                if second:
                    prob = jnp.exp(s_old[rows, :] - top)
                    sum8 += fold(prob, jnp.sum)
                    e_now[rows, :BLOCK] = prob.astype(BF)
                    e_now[rows, BLOCK:] = (prob * (score[:, BLOCK:] - terms)).astype(BF)
            if c > 0 and third:
                rows = slice((c - 1) * CHUNK, c * CHUNK)
                both = e_old[rows, :]
                acc[rows, :] += dot(both, gweights)
                query_grad += dot(keys_t[:, rows], both[:, BLOCK:])
        if third:
            query_grad = query_grad * (factor * (HD**-0.5))
            query_grad += jnp.where((j - 2) == offset, stat_ref[8:, :], 0.0)
            dq_ref[j - 2] = query_grad.astype(BF)
        if first:
            top = jnp.max(top8, axis=0, keepdims=True)
            st_now[0:1, :] = jnp.where(j == offset, stat_ref[0:1, :], top)
        if second:
            total = jnp.sum(sum8, axis=0, keepdims=True)
            st_old[1:2, :] = jnp.where((j - 1) == offset, stat_ref[1:2, :], 1.0 / total)

    step(0, 0, True, False, False)
    step(1, 1, True, True, False)
    acc[...] = jnp.zeros_like(acc)

    def pair(i, carry):
        step(2 * i, 0, True, True, True)
        step(2 * i + 1, 1, True, True, True)
        return carry

    lax.fori_loop(1, NB // 2, pair, 0)
    step(NB, 0, False, True, True)
    step(NB + 1, 1, False, False, True)


def near_part(offsets, kv, qg, stat):
    return pl.pallas_call(
        near_kernel,
        out_shape=(
            jax.ShapeDtypeStruct((NB, HD, BLOCK), BF),
            jax.ShapeDtypeStruct((SEG, 2 * HD), F32),
        ),
        in_specs=[SMEM] + [VMEM] * 3,
        out_specs=(VMEM, VMEM),
        scratch_shapes=[
            pltpu.VMEM((HD, SEG), BF),
            pltpu.VMEM((NB, 2 * HD, BLOCK), BF),
            pltpu.VMEM((SEG, BLOCK), F32),
            pltpu.VMEM((SEG, BLOCK), F32),
            pltpu.VMEM((SEG, 2 * BLOCK), BF),
            pltpu.VMEM((SEG, 2 * BLOCK), BF),
            pltpu.VMEM((8, BLOCK), F32),
            pltpu.VMEM((8, BLOCK), F32),
        ],
        compiler_params=params(28),
        cost_estimate=cost(15 * 10**9, 4 * 10**6, SEG * SEG),
        name="near_part",
    )(offsets, kv, qg, stat)


def finish_kernel(offs_ref, dq_ref, acc, parts_ref, out_ref):
    offset = offs_ref[lax.axis_index("inner")]
    for b in range(NB):
        out_ref[b, :BLOCK, :] = acc[b * BLOCK : (b + 1) * BLOCK, :].astype(BF)
        out_ref[b, BLOCK:, :] = dq_ref[b]
    total = acc[pl.ds(pl.multiple_of(offset * BLOCK, BLOCK), BLOCK), :]
    for n in range(NB):
        total += parts_ref[n].astype(F32)
    out_ref[offset, :BLOCK, :] = total.astype(BF)


def finish(offsets, dq, sums, parts):
    return pl.pallas_call(
        finish_kernel,
        out_shape=jax.ShapeDtypeStruct((NB, OUT_ROWS, BLOCK), BF),
        in_specs=[SMEM, VMEM, VMEM, VMEM],
        out_specs=VMEM,
        compiler_params=params(16),
        cost_estimate=cost(10**6, 10**6),
        name="finish_picked",
    )(offsets, dq, sums, parts)


def unpack_kernel(in_ref, q_out, k_out, v_out, q_ref, k_ref, v_ref, sems):
    outs = []
    for n in range(GROUPS):
        for pair in range(n * GROUP // 2, (n + 1) * GROUP // 2):
            cols = slice(pair * 2 * HD, (pair + 1) * 2 * HD)
            one, two = in_ref[2 * pair, :BLOCK, :], in_ref[2 * pair + 1, :BLOCK, :]
            k_ref[:, cols] = jnp.concatenate([one[:, :HD], two[:, :HD]], axis=1)
            v_ref[:, cols] = jnp.concatenate([one[:, HD:], two[:, HD:]], axis=1)
            turned = jnp.concatenate(
                [in_ref[2 * pair, BLOCK:, :], in_ref[2 * pair + 1, BLOCK:, :]], axis=0
            )
            q_ref[:, cols] = turned.T
        cols = pl.ds(n * GROUP_COLS, GROUP_COLS)
        pairs = [(ref.at[:, cols], out.at[:, cols]) for ref, out in ((q_ref, q_out), (k_ref, k_out), (v_ref, v_out))]
        outs += fetch(pairs, sems.at[n])
    for out in outs:
        out.wait()


def unpack(block):
    shape = jax.ShapeDtypeStruct((BLOCK, HEADS * HD), BF)
    return pl.pallas_call(
        unpack_kernel,
        out_shape=(shape, shape, shape),
        in_specs=[VMEM],
        out_specs=(ANY, ANY, ANY),
        scratch_shapes=[pltpu.VMEM((BLOCK, HEADS * HD), BF)] * 3
        + [pltpu.SemaphoreType.DMA((GROUPS, 3))],
        compiler_params=params(16),
        cost_estimate=cost(10**6, 2 * 10**6),
        name="unpack_heads",
    )(block)


def exchange(array, axis):
    return lax.all_to_all(array, axis, split_axis=0, concat_axis=0, tiled=True)


def spread(block):
    def ring(step, along_x):
        pairs = []
        for x in range(RING):
            for y in range(RING):
                source = (x + step) % RING * RING + y if along_x else x * RING + (y + step) % RING
                pairs.append((source, x * RING + y))
        return pairs

    row = jnp.stack([block] + [lax.ppermute(block, "outer", ring(n, False)) for n in (1, 2, 3)])
    return [row] + [lax.ppermute(row, "outer", ring(n, True)) for n in (1, 2, 3)]


def on_device(queries, keys, values, saved_out, out_grad, offsets):
    kv = exchange(pack_kv(keys, values), "inner")
    qg = pack_qg(queries, saved_out, out_grad)
    fars = spread(pick(offsets, kv))
    qg = exchange(qg, "inner")
    near_stat = prepare(offsets, kv, qg)
    parts, stat = far_part(offsets, qg, near_stat, fars)
    parts = exchange(parts, "outer")
    dq, sums = near_part(offsets, kv, qg, stat)
    whole = finish(offsets, dq, sums, parts)
    return unpack(exchange(whole, "inner"))


def solution(mesh):
    rows = P(("outer", "inner"), None)
    return jax.shard_map(
        on_device,
        mesh=mesh,
        in_specs=(rows, rows, rows, rows, rows, P()),
        out_specs=(rows, rows, rows),
        check_vma=False,
    )
```

```python
import jax
import jax.numpy as jnp
from jax import lax
from jax.experimental import pallas as pl
from jax.experimental.pallas import tpu as pltpu
from jax.sharding import PartitionSpec as P

HEADS = 16
HD = 64
BLOCK = 128
NB = 16
RING = 4
GROUP = 8
GROUPS = HEADS // GROUP
GROUP_COLS = GROUP * HD
SEG = NB * BLOCK
CHUNK = 256
BF = jnp.bfloat16
F32 = jnp.float32
KV_ORDER = (1, 0)
QG_ORDER = (1, 0)
OUT_ORDER = (-1, 15)
VMEM = pl.BlockSpec(memory_space=pltpu.VMEM)
SMEM = pl.BlockSpec(memory_space=pltpu.SMEM)
QG_ROWS = BLOCK + 16
OUT_ROWS = BLOCK + HD


def params(mib):
    return pltpu.CompilerParams(vmem_limit_bytes=mib * 1024 * 1024)


def cost(flops, nbytes, exps=0):
    return pl.CostEstimate(flops=flops, bytes_accessed=nbytes, transcendentals=exps)


def entry(order, i):
    sign, first = order
    return (sign * (i - first) + 2 * HEADS) % HEADS


def dot(a, b):
    return jnp.dot(a, b, preferred_element_type=F32)


def dot_nt(a, b):
    return lax.dot_general(a, b, (((1,), (1,)), ((), ())), preferred_element_type=F32)


def split3(x):
    high = x.astype(BF)
    rest = x - high.astype(F32)
    mid = rest.astype(BF)
    low = (rest - mid.astype(F32)).astype(BF)
    return high, mid, low


ANY = pl.BlockSpec(memory_space=pl.ANY)


def fetch(pairs, sems):
    copies = [
        pltpu.make_async_copy(source, target, sems.at[n]) for n, (source, target) in enumerate(pairs)
    ]
    for copy in copies:
        copy.start()
    return copies


def half_of(ref, head):
    start = head * HD
    return ref[:, start : start + HD]


def pack_kv_kernel(k_in, v_in, kv_out, k_ref, v_ref, kv_ref, sems, out_sems):
    copies = []
    for n in range(GROUPS):
        cols = pl.ds(n * GROUP_COLS, GROUP_COLS)
        pairs = ((k_in.at[:, cols], k_ref.at[:, cols]), (v_in.at[:, cols], v_ref.at[:, cols]))
        copies.append(fetch(pairs, sems.at[n]))
    outs = []
    for n in range(GROUPS):
        group = range(n * GROUP, (n + 1) * GROUP)
        for copy in copies[n]:
            copy.wait()
        for head in group:
            kv_ref[entry(KV_ORDER, head)] = jnp.concatenate(
                [half_of(k_ref, head), half_of(v_ref, head)], axis=1
            )
        heads = pl.ds(min(entry(KV_ORDER, head) for head in group), GROUP)
        outs.append(pltpu.make_async_copy(kv_ref.at[heads], kv_out.at[heads], out_sems.at[n]))
        outs[n].start()
    for out in outs:
        out.wait()


def pack_kv(keys, values):
    return pl.pallas_call(
        pack_kv_kernel,
        out_shape=jax.ShapeDtypeStruct((HEADS, BLOCK, 2 * HD), BF),
        in_specs=[ANY] * 2,
        out_specs=ANY,
        scratch_shapes=[pltpu.VMEM((BLOCK, HEADS * HD), BF)] * 2
        + [
            pltpu.VMEM((HEADS, BLOCK, 2 * HD), BF),
            pltpu.SemaphoreType.DMA((GROUPS, 2)),
            pltpu.SemaphoreType.DMA((GROUPS,)),
        ],
        compiler_params=params(60),
        cost_estimate=cost(10**6, 10**6),
        name="pack_keys_values",
    )(keys, values)


def pack_qg_kernel(q_in, o_in, g_in, qg_ref, q_ref, o_ref, g_ref, sems):
    copies = fetch(((g_in, g_ref), (o_in, o_ref), (q_in, q_ref)), sems)
    copies[0].wait()
    copies[1].wait()
    head_of = lax.broadcasted_iota(jnp.int32, (HEADS, HEADS * HD), 1) // HD
    mine = head_of == lax.broadcasted_iota(jnp.int32, (HEADS, HEADS * HD), 0)
    ones = jnp.where(mine, 1.0, 0.0).astype(BF)
    product = g_ref[...].astype(F32) * o_ref[...].astype(F32)
    high = product.astype(BF)
    low = (product - high.astype(F32)).astype(BF)
    terms = dot_nt(ones, high) + dot_nt(ones, low)
    parts = [part.astype(F32) for part in split3(terms)]
    row = lax.broadcasted_iota(jnp.int32, (16, BLOCK), 0)
    copies[2].wait()
    for head in range(HEADS):
        q = (half_of(q_ref, head).astype(F32) * (HD**-0.5)).astype(BF)
        place = entry(QG_ORDER, head)
        qg_ref[place, :BLOCK, :] = jnp.concatenate([q, half_of(g_ref, head)], axis=1)
        tail = jnp.zeros((16, BLOCK), F32)
        for n, part in enumerate(parts):
            tail = jnp.where(row == n, part[head : head + 1, :], tail)
        qg_ref[place, BLOCK:, :] = tail.astype(BF)


def pack_qg(queries, saved_out, out_grad):
    return pl.pallas_call(
        pack_qg_kernel,
        out_shape=jax.ShapeDtypeStruct((HEADS, QG_ROWS, 2 * HD), BF),
        in_specs=[ANY] * 3,
        out_specs=VMEM,
        scratch_shapes=[pltpu.VMEM((BLOCK, HEADS * HD), BF)] * 3 + [pltpu.SemaphoreType.DMA((3,))],
        compiler_params=params(60),
        cost_estimate=cost(10**7, 2 * 10**6),
        name="pack_queries_grads",
    )(queries, saved_out, out_grad)


def pick_kernel(offs_ref, kv_ref, out_ref):
    out_ref[...] = kv_ref[entry(KV_ORDER, offs_ref[lax.axis_index("inner")])]


def pick(offsets, kv):
    return pl.pallas_call(
        pick_kernel,
        out_shape=jax.ShapeDtypeStruct(kv.shape[1:], kv.dtype),
        in_specs=[SMEM, VMEM],
        out_specs=VMEM,
        compiler_params=params(4),
        cost_estimate=cost(10**3, 10**5),
        name="pick_block",
    )(offsets, kv)


def block_terms(tail):
    tail = tail.astype(F32)
    return tail[0:1, :] + tail[1:2, :] + tail[2:3, :]


def score_weights(q_turned, g_turned):
    zero = jnp.zeros((HD, BLOCK), BF)
    none = zero if q_turned is None else q_turned
    grad = zero if g_turned is None else g_turned
    return jnp.concatenate(
        [jnp.concatenate([none, zero], axis=1), jnp.concatenate([zero, grad], axis=1)], axis=0
    )


def grad_weights(turned, factor):
    scaled = (turned.astype(F32) * factor).T.astype(BF)
    left = lax.broadcasted_iota(jnp.int32, scaled.shape, 1) < HD
    zero = jnp.zeros_like(scaled)
    return jnp.concatenate(
        [jnp.where(left, zero, scaled), jnp.where(left, scaled, zero)], axis=0
    )


def kv_rows(kv_ref, c):
    per = CHUNK // BLOCK
    return kv_ref[c * per : (c + 1) * per].reshape(CHUNK, 2 * HD)


def fold(x, op):
    return op(x.reshape(-1, 8, x.shape[1]), axis=0)


def far_kernel(
    offs_ref, kv_ref, qg_ref, far0, far1, far2, far3, part_ref, stat_ref, near_s, far_s, ed, keys_t
):
    offset = entry(QG_ORDER, offs_ref[lax.axis_index("inner")])
    place = lax.axis_index("outer")
    place_x, place_y = place // RING, place % RING
    odd = lax.axis_index("inner") % 2
    fars = (far0, far1, far2, far3)

    def far_rows(c):
        per = CHUNK // BLOCK
        a, b = divmod(c * per, RING)
        return fars[a][b : b + per].reshape(CHUNK, 2 * HD)

    terms = block_terms(qg_ref[offset, BLOCK:, :])
    turned = qg_ref[offset, :BLOCK, :].T
    weights = score_weights(turned[:HD, :], turned[HD:, :])
    top8 = jnp.full((8, BLOCK), -jnp.inf, F32)
    for c in range(SEG // CHUNK):
        rows = slice(c * CHUNK, (c + 1) * CHUNK)
        near = dot(kv_rows(kv_ref, c), weights[:, :BLOCK])
        near_s[rows, :] = near
        far = dot(far_rows(c), weights)
        far_s[rows, :] = far
        keys_t[:, rows] = far_rows(c).T[:HD, :]
        top8 = jnp.maximum(top8, jnp.maximum(fold(near, jnp.max), fold(far[:, :BLOCK], jnp.max)))
    top = jnp.max(top8, axis=0, keepdims=True)
    sum8 = jnp.zeros((8, BLOCK), F32)
    for c in range(SEG // CHUNK):
        rows = slice(c * CHUNK, (c + 1) * CHUNK)
        prob = jnp.exp(far_s[rows, :BLOCK] - top)
        sum8 += fold(prob, jnp.sum) + fold(jnp.exp(near_s[rows, :] - top), jnp.sum)
        ed[rows, :BLOCK] = prob.astype(BF)
        ed[rows, BLOCK:] = (prob * (far_s[rows, BLOCK:] - terms)).astype(BF)
    factor = 1.0 / jnp.sum(sum8, axis=0, keepdims=True)
    second = grad_weights(turned, factor)
    query_grad = jnp.zeros((HD, BLOCK), F32)
    for c in range(SEG // CHUNK):
        rows = slice(c * CHUNK, (c + 1) * CHUNK)
        both = ed[rows, :]
        grads = dot(both, second).astype(BF)
        for n in range(CHUNK // BLOCK):
            a, b = divmod(c * CHUNK // BLOCK + n, RING)
            step_x = b + odd * (a - b)
            owner = (place_x + step_x) % RING * RING + (place_y + a + b - step_x) % RING
            part_ref[owner] = grads[n * BLOCK : (n + 1) * BLOCK, :]
        query_grad += dot(keys_t[:, rows], both[:, BLOCK:])
    stat_ref[0:1, :] = top
    stat_ref[1:2, :] = factor
    stat_ref[8:, :] = query_grad * factor * (HD**-0.5)


def far_part(offsets, kv, qg, fars):
    return pl.pallas_call(
        far_kernel,
        out_shape=(
            jax.ShapeDtypeStruct((NB, BLOCK, 2 * HD), BF),
            jax.ShapeDtypeStruct((8 + HD, BLOCK), F32),
        ),
        in_specs=[SMEM] + [VMEM] * 6,
        out_specs=(VMEM, VMEM),
        scratch_shapes=[
            pltpu.VMEM((SEG, BLOCK), F32),
            pltpu.VMEM((SEG, 2 * BLOCK), F32),
            pltpu.VMEM((SEG, 2 * BLOCK), BF),
            pltpu.VMEM((HD, SEG), BF),
        ],
        compiler_params=params(20),
        cost_estimate=cost(2 * 10**9, 2 * 10**6),
        name="far_part",
    )(offsets, kv, qg, *fars)


def near_kernel(
    offs_ref, kv_ref, qg_ref, stat_ref, dq_ref, acc, keys_t, turned_ref, s0, s1, e0, e1, st0, st1
):
    offset = entry(QG_ORDER, offs_ref[lax.axis_index("inner")])
    score_refs, grad_refs, stats = (s0, s1), (e0, e1), (st0, st1)
    chunks = SEG // CHUNK
    turned_ref[0] = qg_ref[0, :BLOCK, :].T

    def prepare(c):
        rows = slice(c * CHUNK, (c + 1) * CHUNK)
        keys_t[:, rows] = kv_rows(kv_ref, c).T[:HD, :]
        acc[rows, :] = jnp.zeros((CHUNK, 2 * HD), F32)
        for b in range(max(1, c * NB // chunks), (c + 1) * NB // chunks):
            turned_ref[b] = qg_ref[b, :BLOCK, :].T

    def step(j, slot, first, second, third):
        s_now, s_old = score_refs[slot], score_refs[1 - slot]
        e_now, e_old = grad_refs[1 - slot], grad_refs[slot]
        st_now, st_old = stats[slot], stats[1 - slot]
        top8 = jnp.full((8, BLOCK), -jnp.inf, F32)
        sum8 = jnp.zeros((8, BLOCK), F32)
        query_grad = jnp.zeros((HD, BLOCK), F32)
        if first or second:
            weights = score_weights(
                turned_ref[j, :HD, :] if first else None,
                turned_ref[j - 1, HD:, :] if second else None,
            )
        if second:
            terms = block_terms(qg_ref[j - 1, BLOCK:, :])
            top = st_old[0:1, :]
        if third:
            factor = st_now[1:2, :]
            gweights = grad_weights(turned_ref[j - 2], factor)
        for c in range(chunks + 1):
            if c < chunks and not second and not third:
                prepare(c)
            if c < chunks and (first or second):
                rows = slice(c * CHUNK, (c + 1) * CHUNK)
                score = dot(kv_rows(kv_ref, c), weights)
                if first:
                    s_now[rows, :] = score[:, :BLOCK]
                    top8 = jnp.maximum(top8, fold(score[:, :BLOCK], jnp.max))
                if second:
                    prob = jnp.exp(s_old[rows, :] - top)
                    sum8 += fold(prob, jnp.sum)
                    e_now[rows, :BLOCK] = prob.astype(BF)
                    e_now[rows, BLOCK:] = (prob * (score[:, BLOCK:] - terms)).astype(BF)
            if c > 0 and third:
                rows = slice((c - 1) * CHUNK, c * CHUNK)
                both = e_old[rows, :]
                acc[rows, :] += dot(both, gweights)
                query_grad += dot(keys_t[:, rows], both[:, BLOCK:])
        if third:
            query_grad = query_grad * (factor * (HD**-0.5))
            query_grad += jnp.where((j - 2) == offset, stat_ref[8:, :], 0.0)
            dq_ref[j - 2] = query_grad.astype(BF)
        if first:
            top = jnp.max(top8, axis=0, keepdims=True)
            st_now[0:1, :] = jnp.where(j == offset, stat_ref[0:1, :], top)
        if second:
            total = jnp.sum(sum8, axis=0, keepdims=True)
            st_old[1:2, :] = jnp.where((j - 1) == offset, stat_ref[1:2, :], 1.0 / total)

    step(0, 0, True, False, False)
    step(1, 1, True, True, False)

    def pair(i, carry):
        step(2 * i, 0, True, True, True)
        step(2 * i + 1, 1, True, True, True)
        return carry

    lax.fori_loop(1, NB // 2, pair, 0)
    step(NB, 0, False, True, True)
    step(NB + 1, 1, False, False, True)


def near_part(offsets, kv, qg, stat):
    return pl.pallas_call(
        near_kernel,
        out_shape=(
            jax.ShapeDtypeStruct((NB, HD, BLOCK), BF),
            jax.ShapeDtypeStruct((SEG, 2 * HD), F32),
        ),
        in_specs=[SMEM] + [VMEM] * 3,
        out_specs=(VMEM, VMEM),
        scratch_shapes=[
            pltpu.VMEM((HD, SEG), BF),
            pltpu.VMEM((NB, 2 * HD, BLOCK), BF),
            pltpu.VMEM((SEG, BLOCK), F32),
            pltpu.VMEM((SEG, BLOCK), F32),
            pltpu.VMEM((SEG, 2 * BLOCK), BF),
            pltpu.VMEM((SEG, 2 * BLOCK), BF),
            pltpu.VMEM((8, BLOCK), F32),
            pltpu.VMEM((8, BLOCK), F32),
        ],
        compiler_params=params(28),
        cost_estimate=cost(15 * 10**9, 4 * 10**6, SEG * SEG),
        name="near_part",
    )(offsets, kv, qg, stat)


def finish_kernel(offs_ref, dq_ref, acc, parts_ref, out_ref):
    offset = offs_ref[lax.axis_index("inner")]
    for b in range(NB):
        start = entry(KV_ORDER, b) * BLOCK
        place = entry(OUT_ORDER, b)
        out_ref[place, :BLOCK, :] = acc[start : start + BLOCK, :].astype(BF)
        out_ref[place, BLOCK:, :] = dq_ref[entry(QG_ORDER, b)]
    start = pl.multiple_of(entry(KV_ORDER, offset) * BLOCK, BLOCK)
    total = acc[pl.ds(start, BLOCK), :]
    for n in range(NB):
        total += parts_ref[n].astype(F32)
    out_ref[entry(OUT_ORDER, offset), :BLOCK, :] = total.astype(BF)


def finish(offsets, dq, sums, parts):
    return pl.pallas_call(
        finish_kernel,
        out_shape=jax.ShapeDtypeStruct((NB, OUT_ROWS, BLOCK), BF),
        in_specs=[SMEM, VMEM, VMEM, VMEM],
        out_specs=VMEM,
        compiler_params=params(16),
        cost_estimate=cost(10**6, 10**6),
        name="finish_picked",
    )(offsets, dq, sums, parts)


def unpack_kernel(in_ref, q_out, k_out, v_out, q_ref, k_ref, v_ref, sems):
    outs = []
    for n in range(GROUPS):
        for pair in range(n * GROUP // 2, (n + 1) * GROUP // 2):
            cols = slice(pair * 2 * HD, (pair + 1) * 2 * HD)
            first, second = (in_ref.at[entry(OUT_ORDER, 2 * pair + n)] for n in range(2))
            one, two = first[:BLOCK, :], second[:BLOCK, :]
            k_ref[:, cols] = jnp.concatenate([one[:, :HD], two[:, :HD]], axis=1)
            v_ref[:, cols] = jnp.concatenate([one[:, HD:], two[:, HD:]], axis=1)
            turned = jnp.concatenate([first[BLOCK:, :], second[BLOCK:, :]], axis=0)
            q_ref[:, cols] = turned.T
        cols = pl.ds(n * GROUP_COLS, GROUP_COLS)
        pairs = [(ref.at[:, cols], out.at[:, cols]) for ref, out in ((q_ref, q_out), (k_ref, k_out), (v_ref, v_out))]
        outs += fetch(pairs, sems.at[n])
    for out in outs:
        out.wait()


def unpack(block):
    shape = jax.ShapeDtypeStruct((BLOCK, HEADS * HD), BF)
    return pl.pallas_call(
        unpack_kernel,
        out_shape=(shape, shape, shape),
        in_specs=[VMEM],
        out_specs=(ANY, ANY, ANY),
        scratch_shapes=[pltpu.VMEM((BLOCK, HEADS * HD), BF)] * 3
        + [pltpu.SemaphoreType.DMA((GROUPS, 3))],
        compiler_params=params(16),
        cost_estimate=cost(10**6, 2 * 10**6),
        name="unpack_heads",
    )(block)


def exchange(array, axis, order=None):
    groups = None
    if order is not None:
        sign, first = order
        groups = [[(first + sign * n) % HEADS for n in range(HEADS)]]
    return lax.all_to_all(
        array, axis, split_axis=0, concat_axis=0, tiled=True, axis_index_groups=groups
    )


def spread(block):
    inner_count = lax.axis_size("inner")

    def ring(step, first):
        pairs = []
        for place in range(RING * RING):
            x, y = place // RING, place % RING
            along_y = x * RING + (y + step) % RING
            along_x = (x + step) % RING * RING + y
            for inner in range(inner_count):
                source = along_y if (inner % 2 == 1) == first else along_x
                pairs.append((source * inner_count + inner, place * inner_count + inner))
        return pairs

    def send(array, step, first):
        return lax.ppermute(array, ("outer", "inner"), ring(step, first))

    row = jnp.stack([block] + [send(block, n, True) for n in (1, 2, 3)])
    return [row] + [send(row, n, False) for n in (1, 2, 3)]


def on_device(queries, keys, values, saved_out, out_grad, offsets):
    kv = exchange(pack_kv(keys, values), "inner", KV_ORDER)
    qg = pack_qg(queries, saved_out, out_grad)
    fars = spread(pick(offsets, kv))
    qg = exchange(qg, "inner", QG_ORDER)
    parts, stat = far_part(offsets, kv, qg, fars)
    parts = exchange(parts, "outer")
    dq, sums = near_part(offsets, kv, qg, stat)
    whole = finish(offsets, dq, sums, parts)
    return unpack(exchange(whole, "inner", OUT_ORDER))


def solution(mesh):
    rows = P(("outer", "inner"), None)
    return jax.shard_map(
        on_device,
        mesh=mesh,
        in_specs=(rows, rows, rows, rows, rows, P()),
        out_specs=(rows, rows, rows),
        check_vma=False,
    )
```

```python
import jax
import jax.numpy as jnp
from jax import lax
from jax.experimental import pallas as pl
from jax.experimental.pallas import tpu as pltpu
from jax.sharding import PartitionSpec as P

HEADS = 16
HD = 64
BLOCK = 128
NB = 16
RING = 4
GROUP = 8
GROUPS = HEADS // GROUP
GROUP_COLS = GROUP * HD
SEG = NB * BLOCK
CHUNK = 256
BF = jnp.bfloat16
F32 = jnp.float32
KV_ORDER = (1, 8)
QG_ORDER = (1, 8)
OUT_ORDER = (-1, 15)
VMEM = pl.BlockSpec(memory_space=pltpu.VMEM)
SMEM = pl.BlockSpec(memory_space=pltpu.SMEM)
QG_ROWS = BLOCK + 16
OUT_ROWS = BLOCK + HD


def params(mib):
    return pltpu.CompilerParams(vmem_limit_bytes=mib * 1024 * 1024)


def cost(flops, nbytes, exps=0):
    return pl.CostEstimate(flops=flops, bytes_accessed=nbytes, transcendentals=exps)


def entry(order, i):
    sign, first = order
    return (sign * (i - first) + 2 * HEADS) % HEADS


def dot(a, b):
    return jnp.dot(a, b, preferred_element_type=F32)


def dot_nt(a, b):
    return lax.dot_general(a, b, (((1,), (1,)), ((), ())), preferred_element_type=F32)


def split3(x):
    high = x.astype(BF)
    rest = x - high.astype(F32)
    mid = rest.astype(BF)
    low = (rest - mid.astype(F32)).astype(BF)
    return high, mid, low


ANY = pl.BlockSpec(memory_space=pl.ANY)


def fetch(pairs, sems):
    copies = [
        pltpu.make_async_copy(source, target, sems.at[n]) for n, (source, target) in enumerate(pairs)
    ]
    for copy in copies:
        copy.start()
    return copies


def half_of(ref, head):
    start = head * HD
    return ref[:, start : start + HD]


def pack_kv_kernel(k_in, v_in, kv_out, k_ref, v_ref, kv_ref, sems, out_sems):
    copies = []
    for n in range(GROUPS):
        cols = pl.ds(n * GROUP_COLS, GROUP_COLS)
        pairs = ((k_in.at[:, cols], k_ref.at[:, cols]), (v_in.at[:, cols], v_ref.at[:, cols]))
        copies.append(fetch(pairs, sems.at[n]))
    outs = []
    for n in range(GROUPS):
        group = range(n * GROUP, (n + 1) * GROUP)
        for copy in copies[n]:
            copy.wait()
        for head in group:
            kv_ref[entry(KV_ORDER, head)] = jnp.concatenate(
                [half_of(k_ref, head), half_of(v_ref, head)], axis=1
            )
        heads = pl.ds(min(entry(KV_ORDER, head) for head in group), GROUP)
        outs.append(pltpu.make_async_copy(kv_ref.at[heads], kv_out.at[heads], out_sems.at[n]))
        outs[n].start()
    for out in outs:
        out.wait()


def pack_kv(keys, values):
    return pl.pallas_call(
        pack_kv_kernel,
        out_shape=jax.ShapeDtypeStruct((HEADS, BLOCK, 2 * HD), BF),
        in_specs=[ANY] * 2,
        out_specs=ANY,
        scratch_shapes=[pltpu.VMEM((BLOCK, HEADS * HD), BF)] * 2
        + [
            pltpu.VMEM((HEADS, BLOCK, 2 * HD), BF),
            pltpu.SemaphoreType.DMA((GROUPS, 2)),
            pltpu.SemaphoreType.DMA((GROUPS,)),
        ],
        compiler_params=params(60),
        cost_estimate=cost(10**6, 10**6),
        name="pack_keys_values",
    )(keys, values)


def pack_qg_kernel(q_in, o_in, g_in, qg_ref, q_ref, o_ref, g_ref, sems):
    copies = fetch(((g_in, g_ref), (o_in, o_ref), (q_in, q_ref)), sems)
    copies[0].wait()
    copies[1].wait()
    head_of = lax.broadcasted_iota(jnp.int32, (HEADS, HEADS * HD), 1) // HD
    mine = head_of == lax.broadcasted_iota(jnp.int32, (HEADS, HEADS * HD), 0)
    ones = jnp.where(mine, 1.0, 0.0).astype(BF)
    product = g_ref[...].astype(F32) * o_ref[...].astype(F32)
    high = product.astype(BF)
    low = (product - high.astype(F32)).astype(BF)
    terms = dot_nt(ones, high) + dot_nt(ones, low)
    parts = [part.astype(F32) for part in split3(terms)]
    row = lax.broadcasted_iota(jnp.int32, (16, BLOCK), 0)
    copies[2].wait()
    for head in range(HEADS):
        q = (half_of(q_ref, head).astype(F32) * (HD**-0.5)).astype(BF)
        place = entry(QG_ORDER, head)
        qg_ref[place, :BLOCK, :] = jnp.concatenate([q, half_of(g_ref, head)], axis=1)
        tail = jnp.zeros((16, BLOCK), F32)
        for n, part in enumerate(parts):
            tail = jnp.where(row == n, part[head : head + 1, :], tail)
        qg_ref[place, BLOCK:, :] = tail.astype(BF)


def pack_qg(queries, saved_out, out_grad):
    return pl.pallas_call(
        pack_qg_kernel,
        out_shape=jax.ShapeDtypeStruct((HEADS, QG_ROWS, 2 * HD), BF),
        in_specs=[ANY] * 3,
        out_specs=VMEM,
        scratch_shapes=[pltpu.VMEM((BLOCK, HEADS * HD), BF)] * 3 + [pltpu.SemaphoreType.DMA((3,))],
        compiler_params=params(60),
        cost_estimate=cost(10**7, 2 * 10**6),
        name="pack_queries_grads",
    )(queries, saved_out, out_grad)


def pick_kernel(offs_ref, kv_ref, out_ref):
    out_ref[...] = kv_ref[entry(KV_ORDER, offs_ref[lax.axis_index("inner")])]


def pick(offsets, kv):
    return pl.pallas_call(
        pick_kernel,
        out_shape=jax.ShapeDtypeStruct(kv.shape[1:], kv.dtype),
        in_specs=[SMEM, VMEM],
        out_specs=VMEM,
        compiler_params=params(4),
        cost_estimate=cost(10**3, 10**5),
        name="pick_block",
    )(offsets, kv)


def block_terms(tail):
    tail = tail.astype(F32)
    return tail[0:1, :] + tail[1:2, :] + tail[2:3, :]


def score_weights(q_turned, g_turned):
    zero = jnp.zeros((HD, BLOCK), BF)
    none = zero if q_turned is None else q_turned
    grad = zero if g_turned is None else g_turned
    return jnp.concatenate(
        [jnp.concatenate([none, zero], axis=1), jnp.concatenate([zero, grad], axis=1)], axis=0
    )


def grad_weights(turned, factor):
    scaled = (turned.astype(F32) * factor).T.astype(BF)
    left = lax.broadcasted_iota(jnp.int32, scaled.shape, 1) < HD
    zero = jnp.zeros_like(scaled)
    return jnp.concatenate(
        [jnp.where(left, zero, scaled), jnp.where(left, scaled, zero)], axis=0
    )


def kv_rows(kv_ref, c):
    per = CHUNK // BLOCK
    return kv_ref[c * per : (c + 1) * per].reshape(CHUNK, 2 * HD)


def fold(x, op):
    return op(x.reshape(-1, 8, x.shape[1]), axis=0)


def far_kernel(
    offs_ref, kv_ref, qg_ref, far0, far1, far2, far3, part_ref, stat_ref, near_s, far_s, ed, keys_t
):
    offset = entry(QG_ORDER, offs_ref[lax.axis_index("inner")])
    place = lax.axis_index("outer")
    place_x, place_y = place // RING, place % RING
    odd = lax.axis_index("inner") % 2
    fars = (far0, far1, far2, far3)

    def far_rows(c):
        per = CHUNK // BLOCK
        a, b = divmod(c * per, RING)
        return fars[a][b : b + per].reshape(CHUNK, 2 * HD)

    terms = block_terms(qg_ref[offset, BLOCK:, :])
    turned = qg_ref[offset, :BLOCK, :].T
    weights = score_weights(turned[:HD, :], turned[HD:, :])
    top8 = jnp.full((8, BLOCK), -jnp.inf, F32)
    for c in range(SEG // CHUNK):
        rows = slice(c * CHUNK, (c + 1) * CHUNK)
        near = dot(kv_rows(kv_ref, c), weights[:, :BLOCK])
        near_s[rows, :] = near
        far = dot(far_rows(c), weights)
        far_s[rows, :] = far
        keys_t[:, rows] = far_rows(c).T[:HD, :]
        top8 = jnp.maximum(top8, jnp.maximum(fold(near, jnp.max), fold(far[:, :BLOCK], jnp.max)))
    top = jnp.max(top8, axis=0, keepdims=True)
    sum8 = jnp.zeros((8, BLOCK), F32)
    for c in range(SEG // CHUNK):
        rows = slice(c * CHUNK, (c + 1) * CHUNK)
        prob = jnp.exp(far_s[rows, :BLOCK] - top)
        sum8 += fold(prob, jnp.sum) + fold(jnp.exp(near_s[rows, :] - top), jnp.sum)
        ed[rows, :BLOCK] = prob.astype(BF)
        ed[rows, BLOCK:] = (prob * (far_s[rows, BLOCK:] - terms)).astype(BF)
    factor = 1.0 / jnp.sum(sum8, axis=0, keepdims=True)
    second = grad_weights(turned, factor)
    query_grad = jnp.zeros((HD, BLOCK), F32)
    for c in range(SEG // CHUNK):
        rows = slice(c * CHUNK, (c + 1) * CHUNK)
        both = ed[rows, :]
        grads = dot(both, second).astype(BF)
        for n in range(CHUNK // BLOCK):
            a, b = divmod(c * CHUNK // BLOCK + n, RING)
            step_x = b + odd * (a - b)
            owner = (place_x + step_x) % RING * RING + (place_y + a + b - step_x) % RING
            part_ref[owner] = grads[n * BLOCK : (n + 1) * BLOCK, :]
        query_grad += dot(keys_t[:, rows], both[:, BLOCK:])
    stat_ref[0:1, :] = top
    stat_ref[1:2, :] = factor
    stat_ref[8:, :] = query_grad * factor * (HD**-0.5)


def far_part(offsets, kv, qg, fars):
    return pl.pallas_call(
        far_kernel,
        out_shape=(
            jax.ShapeDtypeStruct((NB, BLOCK, 2 * HD), BF),
            jax.ShapeDtypeStruct((8 + HD, BLOCK), F32),
        ),
        in_specs=[SMEM] + [VMEM] * 6,
        out_specs=(VMEM, VMEM),
        scratch_shapes=[
            pltpu.VMEM((SEG, BLOCK), F32),
            pltpu.VMEM((SEG, 2 * BLOCK), F32),
            pltpu.VMEM((SEG, 2 * BLOCK), BF),
            pltpu.VMEM((HD, SEG), BF),
        ],
        compiler_params=params(20),
        cost_estimate=cost(2 * 10**9, 2 * 10**6),
        name="far_part",
    )(offsets, kv, qg, *fars)


def near_kernel(
    offs_ref, kv_ref, qg_ref, stat_ref, dq_ref, acc, keys_t, turned_ref, s0, s1, e0, e1, st0, st1
):
    offset = entry(QG_ORDER, offs_ref[lax.axis_index("inner")])
    score_refs, grad_refs, stats = (s0, s1), (e0, e1), (st0, st1)
    chunks = SEG // CHUNK
    turned_ref[0] = qg_ref[0, :BLOCK, :].T

    def prepare(c):
        rows = slice(c * CHUNK, (c + 1) * CHUNK)
        keys_t[:, rows] = kv_rows(kv_ref, c).T[:HD, :]
        acc[rows, :] = jnp.zeros((CHUNK, 2 * HD), F32)
        for b in range(max(1, c * NB // chunks), (c + 1) * NB // chunks):
            turned_ref[b] = qg_ref[b, :BLOCK, :].T

    def step(j, slot, first, second, third):
        s_now, s_old = score_refs[slot], score_refs[1 - slot]
        e_now, e_old = grad_refs[1 - slot], grad_refs[slot]
        st_now, st_old = stats[slot], stats[1 - slot]
        top8 = jnp.full((8, BLOCK), -jnp.inf, F32)
        sum8 = jnp.zeros((8, BLOCK), F32)
        query_grad = jnp.zeros((HD, BLOCK), F32)
        if first or second:
            weights = score_weights(
                turned_ref[j, :HD, :] if first else None,
                turned_ref[j - 1, HD:, :] if second else None,
            )
        if second:
            terms = block_terms(qg_ref[j - 1, BLOCK:, :])
            top = st_old[0:1, :]
        if third:
            factor = st_now[1:2, :]
            gweights = grad_weights(turned_ref[j - 2], factor)
        for c in range(chunks + 1):
            if c < chunks and not second and not third:
                prepare(c)
            if c < chunks and (first or second):
                rows = slice(c * CHUNK, (c + 1) * CHUNK)
                score = dot(kv_rows(kv_ref, c), weights)
                if first:
                    s_now[rows, :] = score[:, :BLOCK]
                    top8 = jnp.maximum(top8, fold(score[:, :BLOCK], jnp.max))
                if second:
                    prob = jnp.exp(s_old[rows, :] - top)
                    sum8 += fold(prob, jnp.sum)
                    e_now[rows, :BLOCK] = prob.astype(BF)
                    e_now[rows, BLOCK:] = (prob * (score[:, BLOCK:] - terms)).astype(BF)
            if c > 0 and third:
                rows = slice((c - 1) * CHUNK, c * CHUNK)
                both = e_old[rows, :]
                acc[rows, :] += dot(both, gweights)
                query_grad += dot(keys_t[:, rows], both[:, BLOCK:])
        if third:
            query_grad = query_grad * (factor * (HD**-0.5))
            query_grad += jnp.where((j - 2) == offset, stat_ref[8:, :], 0.0)
            dq_ref[j - 2] = query_grad.astype(BF)
        if first:
            top = jnp.max(top8, axis=0, keepdims=True)
            st_now[0:1, :] = jnp.where(j == offset, stat_ref[0:1, :], top)
        if second:
            total = jnp.sum(sum8, axis=0, keepdims=True)
            st_old[1:2, :] = jnp.where((j - 1) == offset, stat_ref[1:2, :], 1.0 / total)

    step(0, 0, True, False, False)
    step(1, 1, True, True, False)

    def pair(i, carry):
        step(2 * i, 0, True, True, True)
        step(2 * i + 1, 1, True, True, True)
        return carry

    lax.fori_loop(1, NB // 2, pair, 0)
    step(NB, 0, False, True, True)
    step(NB + 1, 1, False, False, True)


def near_part(offsets, kv, qg, stat):
    return pl.pallas_call(
        near_kernel,
        out_shape=(
            jax.ShapeDtypeStruct((NB, HD, BLOCK), BF),
            jax.ShapeDtypeStruct((SEG, 2 * HD), F32),
        ),
        in_specs=[SMEM] + [VMEM] * 3,
        out_specs=(VMEM, VMEM),
        scratch_shapes=[
            pltpu.VMEM((HD, SEG), BF),
            pltpu.VMEM((NB, 2 * HD, BLOCK), BF),
            pltpu.VMEM((SEG, BLOCK), F32),
            pltpu.VMEM((SEG, BLOCK), F32),
            pltpu.VMEM((SEG, 2 * BLOCK), BF),
            pltpu.VMEM((SEG, 2 * BLOCK), BF),
            pltpu.VMEM((8, BLOCK), F32),
            pltpu.VMEM((8, BLOCK), F32),
        ],
        compiler_params=params(28),
        cost_estimate=cost(15 * 10**9, 4 * 10**6, SEG * SEG),
        name="near_part",
    )(offsets, kv, qg, stat)


def finish_kernel(offs_ref, dq_ref, acc, parts_ref, out_ref):
    offset = offs_ref[lax.axis_index("inner")]
    for b in range(NB):
        start = entry(KV_ORDER, b) * BLOCK
        place = entry(OUT_ORDER, b)
        out_ref[place, :BLOCK, :] = acc[start : start + BLOCK, :].astype(BF)
        out_ref[place, BLOCK:, :] = dq_ref[entry(QG_ORDER, b)]
    start = pl.multiple_of(entry(KV_ORDER, offset) * BLOCK, BLOCK)
    total = acc[pl.ds(start, BLOCK), :]
    for n in range(NB):
        total += parts_ref[n].astype(F32)
    out_ref[entry(OUT_ORDER, offset), :BLOCK, :] = total.astype(BF)


def finish(offsets, dq, sums, parts):
    return pl.pallas_call(
        finish_kernel,
        out_shape=jax.ShapeDtypeStruct((NB, OUT_ROWS, BLOCK), BF),
        in_specs=[SMEM, VMEM, VMEM, VMEM],
        out_specs=VMEM,
        compiler_params=params(16),
        cost_estimate=cost(10**6, 10**6),
        name="finish_picked",
    )(offsets, dq, sums, parts)


def unpack_kernel(in_ref, q_out, k_out, v_out, q_ref, k_ref, v_ref, sems):
    outs = []
    for n in range(GROUPS):
        for pair in range(n * GROUP // 2, (n + 1) * GROUP // 2):
            cols = slice(pair * 2 * HD, (pair + 1) * 2 * HD)
            first, second = (in_ref.at[entry(OUT_ORDER, 2 * pair + n)] for n in range(2))
            one, two = first[:BLOCK, :], second[:BLOCK, :]
            k_ref[:, cols] = jnp.concatenate([one[:, :HD], two[:, :HD]], axis=1)
            v_ref[:, cols] = jnp.concatenate([one[:, HD:], two[:, HD:]], axis=1)
            turned = jnp.concatenate([first[BLOCK:, :], second[BLOCK:, :]], axis=0)
            q_ref[:, cols] = turned.T
        cols = pl.ds(n * GROUP_COLS, GROUP_COLS)
        pairs = [(ref.at[:, cols], out.at[:, cols]) for ref, out in ((q_ref, q_out), (k_ref, k_out), (v_ref, v_out))]
        outs += fetch(pairs, sems.at[n])
    for out in outs:
        out.wait()


def unpack(block):
    shape = jax.ShapeDtypeStruct((BLOCK, HEADS * HD), BF)
    return pl.pallas_call(
        unpack_kernel,
        out_shape=(shape, shape, shape),
        in_specs=[VMEM],
        out_specs=(ANY, ANY, ANY),
        scratch_shapes=[pltpu.VMEM((BLOCK, HEADS * HD), BF)] * 3
        + [pltpu.SemaphoreType.DMA((GROUPS, 3))],
        compiler_params=params(16),
        cost_estimate=cost(10**6, 2 * 10**6),
        name="unpack_heads",
    )(block)


def exchange(array, axis, order=None):
    groups = None
    if order is not None:
        sign, first = order
        groups = [[(first + sign * n) % HEADS for n in range(HEADS)]]
    return lax.all_to_all(
        array, axis, split_axis=0, concat_axis=0, tiled=True, axis_index_groups=groups
    )


def spread(block):
    inner_count = lax.axis_size("inner")

    def ring(step, first):
        pairs = []
        for place in range(RING * RING):
            x, y = place // RING, place % RING
            along_y = x * RING + (y + step) % RING
            along_x = (x + step) % RING * RING + y
            for inner in range(inner_count):
                source = along_y if (inner % 2 == 1) == first else along_x
                pairs.append((source * inner_count + inner, place * inner_count + inner))
        return pairs

    def send(array, step, first):
        return lax.ppermute(array, ("outer", "inner"), ring(step, first))

    row = jnp.stack([block] + [send(block, n, True) for n in (1, 2, 3)])
    return [row] + [send(row, n, False) for n in (1, 2, 3)]


def on_device(queries, keys, values, saved_out, out_grad, offsets):
    kv = exchange(pack_kv(keys, values), "inner", KV_ORDER)
    qg = pack_qg(queries, saved_out, out_grad)
    fars = spread(pick(offsets, kv))
    qg = exchange(qg, "inner", QG_ORDER)
    parts, stat = far_part(offsets, kv, qg, fars)
    parts = exchange(parts, "outer")
    dq, sums = near_part(offsets, kv, qg, stat)
    whole = finish(offsets, dq, sums, parts)
    return unpack(exchange(whole, "inner", OUT_ORDER))


def solution(mesh):
    rows = P(("outer", "inner"), None)
    return jax.shard_map(
        on_device,
        mesh=mesh,
        in_specs=(rows, rows, rows, rows, rows, P()),
        out_specs=(rows, rows, rows),
        check_vma=False,
    )
```

```python
import jax
import jax.numpy as jnp
from jax import lax
from jax.experimental import pallas as pl
from jax.experimental.pallas import tpu as pltpu
from jax.sharding import PartitionSpec as P

HEADS = 16
HD = 64
BLOCK = 128
NB = 16
RING = 4
GROUP = 8
GROUPS = HEADS // GROUP
GROUP_COLS = GROUP * HD
SEG = NB * BLOCK
CHUNK = 256
BF = jnp.bfloat16
F32 = jnp.float32
KV_ORDER = (1, 8)
QG_ORDER = (1, 8)
OUT_ORDER = (-1, 15)
VMEM = pl.BlockSpec(memory_space=pltpu.VMEM)
SMEM = pl.BlockSpec(memory_space=pltpu.SMEM)
QG_ROWS = BLOCK + 16
OUT_ROWS = BLOCK + HD


def params(mib):
    return pltpu.CompilerParams(vmem_limit_bytes=mib * 1024 * 1024)


def cost(flops, nbytes, exps=0):
    return pl.CostEstimate(flops=flops, bytes_accessed=nbytes, transcendentals=exps)


def entry(order, i):
    sign, first = order
    return (sign * (i - first) + 2 * HEADS) % HEADS


def dot(a, b):
    return jnp.dot(a, b, preferred_element_type=F32)


def dot_nt(a, b):
    return lax.dot_general(a, b, (((1,), (1,)), ((), ())), preferred_element_type=F32)


def split3(x):
    high = x.astype(BF)
    rest = x - high.astype(F32)
    mid = rest.astype(BF)
    low = (rest - mid.astype(F32)).astype(BF)
    return high, mid, low


ANY = pl.BlockSpec(memory_space=pl.ANY)


def fetch(pairs, sems):
    copies = [
        pltpu.make_async_copy(source, target, sems.at[n]) for n, (source, target) in enumerate(pairs)
    ]
    for copy in copies:
        copy.start()
    return copies


def half_of(ref, head):
    start = head * HD
    return ref[:, start : start + HD]


def pack_kv_kernel(k_in, v_in, kv_out, k_ref, v_ref, kv_ref, sems, out_sems):
    copies = []
    for n in range(GROUPS):
        cols = pl.ds(n * GROUP_COLS, GROUP_COLS)
        pairs = ((k_in.at[:, cols], k_ref.at[:, cols]), (v_in.at[:, cols], v_ref.at[:, cols]))
        copies.append(fetch(pairs, sems.at[n]))
    outs = []
    for n in range(GROUPS):
        group = range(n * GROUP, (n + 1) * GROUP)
        for copy in copies[n]:
            copy.wait()
        for head in group:
            kv_ref[entry(KV_ORDER, head)] = jnp.concatenate(
                [half_of(k_ref, head), half_of(v_ref, head)], axis=1
            )
        heads = pl.ds(min(entry(KV_ORDER, head) for head in group), GROUP)
        outs.append(pltpu.make_async_copy(kv_ref.at[heads], kv_out.at[heads], out_sems.at[n]))
        outs[n].start()
    for out in outs:
        out.wait()


def pack_kv(keys, values):
    return pl.pallas_call(
        pack_kv_kernel,
        out_shape=jax.ShapeDtypeStruct((HEADS, BLOCK, 2 * HD), BF),
        in_specs=[ANY] * 2,
        out_specs=ANY,
        scratch_shapes=[pltpu.VMEM((BLOCK, HEADS * HD), BF)] * 2
        + [
            pltpu.VMEM((HEADS, BLOCK, 2 * HD), BF),
            pltpu.SemaphoreType.DMA((GROUPS, 2)),
            pltpu.SemaphoreType.DMA((GROUPS,)),
        ],
        compiler_params=params(60),
        cost_estimate=cost(10**6, 10**6),
        name="pack_keys_values",
    )(keys, values)


def pack_qg_kernel(q_in, o_in, g_in, qg_ref, q_ref, o_ref, g_ref, sems):
    copies = fetch(((g_in, g_ref), (o_in, o_ref), (q_in, q_ref)), sems)
    copies[0].wait()
    copies[1].wait()
    head_of = lax.broadcasted_iota(jnp.int32, (HEADS, HEADS * HD), 1) // HD
    mine = head_of == lax.broadcasted_iota(jnp.int32, (HEADS, HEADS * HD), 0)
    ones = jnp.where(mine, 1.0, 0.0).astype(BF)
    product = g_ref[...].astype(F32) * o_ref[...].astype(F32)
    high = product.astype(BF)
    low = (product - high.astype(F32)).astype(BF)
    terms = dot_nt(ones, high) + dot_nt(ones, low)
    parts = [part.astype(F32) for part in split3(terms)]
    row = lax.broadcasted_iota(jnp.int32, (16, BLOCK), 0)
    copies[2].wait()
    for head in range(HEADS):
        q = (half_of(q_ref, head).astype(F32) * (HD**-0.5)).astype(BF)
        place = entry(QG_ORDER, head)
        qg_ref[place, :BLOCK, :] = jnp.concatenate([q, half_of(g_ref, head)], axis=1)
        tail = jnp.zeros((16, BLOCK), F32)
        for n, part in enumerate(parts):
            tail = jnp.where(row == n, part[head : head + 1, :], tail)
        qg_ref[place, BLOCK:, :] = tail.astype(BF)


def pack_qg(queries, saved_out, out_grad):
    return pl.pallas_call(
        pack_qg_kernel,
        out_shape=jax.ShapeDtypeStruct((HEADS, QG_ROWS, 2 * HD), BF),
        in_specs=[ANY] * 3,
        out_specs=VMEM,
        scratch_shapes=[pltpu.VMEM((BLOCK, HEADS * HD), BF)] * 3 + [pltpu.SemaphoreType.DMA((3,))],
        compiler_params=params(60),
        cost_estimate=cost(10**7, 2 * 10**6),
        name="pack_queries_grads",
    )(queries, saved_out, out_grad)


def pick_kernel(offs_ref, kv_ref, out_ref):
    out_ref[...] = kv_ref[entry(KV_ORDER, offs_ref[lax.axis_index("inner")])]


def pick(offsets, kv):
    return pl.pallas_call(
        pick_kernel,
        out_shape=jax.ShapeDtypeStruct(kv.shape[1:], kv.dtype),
        in_specs=[SMEM, VMEM],
        out_specs=VMEM,
        compiler_params=params(4),
        cost_estimate=cost(10**3, 10**5),
        name="pick_block",
    )(offsets, kv)


def block_terms(tail):
    tail = tail.astype(F32)
    return tail[0:1, :] + tail[1:2, :] + tail[2:3, :]


def score_weights(q_turned, g_turned):
    zero = jnp.zeros((HD, BLOCK), BF)
    none = zero if q_turned is None else q_turned
    grad = zero if g_turned is None else g_turned
    return jnp.concatenate(
        [jnp.concatenate([none, zero], axis=1), jnp.concatenate([zero, grad], axis=1)], axis=0
    )


def grad_weights(turned, factor):
    scaled = (turned.astype(F32) * factor).T.astype(BF)
    left = lax.broadcasted_iota(jnp.int32, scaled.shape, 1) < HD
    zero = jnp.zeros_like(scaled)
    return jnp.concatenate(
        [jnp.where(left, zero, scaled), jnp.where(left, scaled, zero)], axis=0
    )


def kv_rows(kv_ref, c):
    per = CHUNK // BLOCK
    return kv_ref[c * per : (c + 1) * per].reshape(CHUNK, 2 * HD)


def fold(x, op):
    return op(x.reshape(-1, 8, x.shape[1]), axis=0)


def prepare_kernel(offs_ref, kv_ref, qg_ref, stat_ref, near_s):
    offset = entry(QG_ORDER, offs_ref[lax.axis_index("inner")])
    weights = qg_ref[offset, :BLOCK, :].T
    top_half = lax.broadcasted_iota(jnp.int32, weights.shape, 0) < HD
    weights = jnp.where(top_half, weights, jnp.zeros_like(weights))
    top8 = jnp.full((8, BLOCK), -jnp.inf, F32)
    for c in range(SEG // CHUNK):
        near = dot(kv_rows(kv_ref, c), weights)
        near_s[c * CHUNK : (c + 1) * CHUNK, :] = near
        top8 = jnp.maximum(top8, fold(near, jnp.max))
    top = jnp.max(top8, axis=0, keepdims=True)
    sum8 = jnp.zeros((8, BLOCK), F32)
    for c in range(SEG // CHUNK):
        sum8 += fold(jnp.exp(near_s[c * CHUNK : (c + 1) * CHUNK, :] - top), jnp.sum)
    stat_ref[0:1, :] = top
    stat_ref[1:2, :] = jnp.sum(sum8, axis=0, keepdims=True)


def prepare(offsets, kv, qg):
    return pl.pallas_call(
        prepare_kernel,
        out_shape=jax.ShapeDtypeStruct((8, BLOCK), F32),
        in_specs=[SMEM, VMEM, VMEM],
        out_specs=VMEM,
        scratch_shapes=[pltpu.VMEM((SEG, BLOCK), F32)],
        compiler_params=params(20),
        cost_estimate=cost(10**9, 2 * 10**6),
        name="prepare_near",
    )(offsets, kv, qg)


def far_kernel(
    offs_ref, qg_ref, near_ref, far0, far1, far2, far3, part_ref, stat_ref, far_s, ed
):
    offset = entry(QG_ORDER, offs_ref[lax.axis_index("inner")])
    place = lax.axis_index("outer")
    place_x, place_y = place // RING, place % RING
    odd = lax.axis_index("inner") % 2
    fars = (far0, far1, far2, far3)

    def far_rows(c):
        per = CHUNK // BLOCK
        a, b = divmod(c * per, RING)
        return fars[a][b : b + per].reshape(CHUNK, 2 * HD)

    terms = block_terms(qg_ref[offset, BLOCK:, :])
    turned = qg_ref[offset, :BLOCK, :].T
    weights = score_weights(turned[:HD, :], turned[HD:, :])
    near_top = near_ref[0:1, :]
    top8 = jnp.broadcast_to(near_top, (8, BLOCK))
    for c in range(SEG // CHUNK):
        rows = slice(c * CHUNK, (c + 1) * CHUNK)
        far = dot(far_rows(c), weights)
        far_s[rows, :] = far
        top8 = jnp.maximum(top8, fold(far[:, :BLOCK], jnp.max))
    top = jnp.max(top8, axis=0, keepdims=True)
    sum8 = jnp.zeros((8, BLOCK), F32)
    for c in range(SEG // CHUNK):
        rows = slice(c * CHUNK, (c + 1) * CHUNK)
        prob = jnp.exp(far_s[rows, :BLOCK] - top)
        sum8 += fold(prob, jnp.sum)
        ed[rows, :BLOCK] = prob.astype(BF)
        ed[rows, BLOCK:] = (prob * (far_s[rows, BLOCK:] - terms)).astype(BF)
    total = jnp.sum(sum8, axis=0, keepdims=True) + near_ref[1:2, :] * jnp.exp(near_top - top)
    factor = 1.0 / total
    second = grad_weights(turned, factor)
    query_grad = jnp.zeros((HD, BLOCK), F32)
    for c in range(SEG // CHUNK):
        rows = slice(c * CHUNK, (c + 1) * CHUNK)
        both = ed[rows, :]
        grads = dot(both, second).astype(BF)
        for n in range(CHUNK // BLOCK):
            a, b = divmod(c * CHUNK // BLOCK + n, RING)
            step_x = b + odd * (a - b)
            owner = (place_x + step_x) % RING * RING + (place_y + a + b - step_x) % RING
            part_ref[owner] = grads[n * BLOCK : (n + 1) * BLOCK, :]
        query_grad += dot(far_rows(c).T[:HD, :], both[:, BLOCK:])
    stat_ref[0:1, :] = top
    stat_ref[1:2, :] = factor
    stat_ref[8:, :] = query_grad * factor * (HD**-0.5)


def far_part(offsets, qg, near_stat, fars):
    return pl.pallas_call(
        far_kernel,
        out_shape=(
            jax.ShapeDtypeStruct((NB, BLOCK, 2 * HD), BF),
            jax.ShapeDtypeStruct((8 + HD, BLOCK), F32),
        ),
        in_specs=[SMEM] + [VMEM] * 6,
        out_specs=(VMEM, VMEM),
        scratch_shapes=[
            pltpu.VMEM((SEG, 2 * BLOCK), F32),
            pltpu.VMEM((SEG, 2 * BLOCK), BF),
        ],
        compiler_params=params(20),
        cost_estimate=cost(2 * 10**9, 2 * 10**6),
        name="far_part",
    )(offsets, qg, near_stat, *fars)


def near_kernel(
    offs_ref, kv_ref, qg_ref, stat_ref, dq_ref, acc, keys_t, turned_ref, s0, s1, e0, e1, st0, st1
):
    offset = entry(QG_ORDER, offs_ref[lax.axis_index("inner")])
    score_refs, grad_refs, stats = (s0, s1), (e0, e1), (st0, st1)
    chunks = SEG // CHUNK
    turned_ref[0] = qg_ref[0, :BLOCK, :].T

    def prepare(c):
        rows = slice(c * CHUNK, (c + 1) * CHUNK)
        keys_t[:, rows] = kv_rows(kv_ref, c).T[:HD, :]
        acc[rows, :] = jnp.zeros((CHUNK, 2 * HD), F32)
        for b in range(max(1, c * NB // chunks), (c + 1) * NB // chunks):
            turned_ref[b] = qg_ref[b, :BLOCK, :].T

    def step(j, slot, first, second, third):
        s_now, s_old = score_refs[slot], score_refs[1 - slot]
        e_now, e_old = grad_refs[1 - slot], grad_refs[slot]
        st_now, st_old = stats[slot], stats[1 - slot]
        top8 = jnp.full((8, BLOCK), -jnp.inf, F32)
        sum8 = jnp.zeros((8, BLOCK), F32)
        query_grad = jnp.zeros((HD, BLOCK), F32)
        if first or second:
            weights = score_weights(
                turned_ref[j, :HD, :] if first else None,
                turned_ref[j - 1, HD:, :] if second else None,
            )
        if second:
            terms = block_terms(qg_ref[j - 1, BLOCK:, :])
            top = st_old[0:1, :]
        if third:
            factor = st_now[1:2, :]
            gweights = grad_weights(turned_ref[j - 2], factor)
        for c in range(chunks + 1):
            if c < chunks and not second and not third:
                prepare(c)
            if c < chunks and (first or second):
                rows = slice(c * CHUNK, (c + 1) * CHUNK)
                score = dot(kv_rows(kv_ref, c), weights)
                if first:
                    s_now[rows, :] = score[:, :BLOCK]
                    top8 = jnp.maximum(top8, fold(score[:, :BLOCK], jnp.max))
                if second:
                    prob = jnp.exp(s_old[rows, :] - top)
                    sum8 += fold(prob, jnp.sum)
                    e_now[rows, :BLOCK] = prob.astype(BF)
                    e_now[rows, BLOCK:] = (prob * (score[:, BLOCK:] - terms)).astype(BF)
            if c > 0 and third:
                rows = slice((c - 1) * CHUNK, c * CHUNK)
                both = e_old[rows, :]
                acc[rows, :] += dot(both, gweights)
                query_grad += dot(keys_t[:, rows], both[:, BLOCK:])
        if third:
            query_grad = query_grad * (factor * (HD**-0.5))
            query_grad += jnp.where((j - 2) == offset, stat_ref[8:, :], 0.0)
            dq_ref[j - 2] = query_grad.astype(BF)
        if first:
            top = jnp.max(top8, axis=0, keepdims=True)
            st_now[0:1, :] = jnp.where(j == offset, stat_ref[0:1, :], top)
        if second:
            total = jnp.sum(sum8, axis=0, keepdims=True)
            st_old[1:2, :] = jnp.where((j - 1) == offset, stat_ref[1:2, :], 1.0 / total)

    step(0, 0, True, False, False)
    step(1, 1, True, True, False)

    def pair(i, carry):
        step(2 * i, 0, True, True, True)
        step(2 * i + 1, 1, True, True, True)
        return carry

    lax.fori_loop(1, NB // 2, pair, 0)
    step(NB, 0, False, True, True)
    step(NB + 1, 1, False, False, True)


def near_part(offsets, kv, qg, stat):
    return pl.pallas_call(
        near_kernel,
        out_shape=(
            jax.ShapeDtypeStruct((NB, HD, BLOCK), BF),
            jax.ShapeDtypeStruct((SEG, 2 * HD), F32),
        ),
        in_specs=[SMEM] + [VMEM] * 3,
        out_specs=(VMEM, VMEM),
        scratch_shapes=[
            pltpu.VMEM((HD, SEG), BF),
            pltpu.VMEM((NB, 2 * HD, BLOCK), BF),
            pltpu.VMEM((SEG, BLOCK), F32),
            pltpu.VMEM((SEG, BLOCK), F32),
            pltpu.VMEM((SEG, 2 * BLOCK), BF),
            pltpu.VMEM((SEG, 2 * BLOCK), BF),
            pltpu.VMEM((8, BLOCK), F32),
            pltpu.VMEM((8, BLOCK), F32),
        ],
        compiler_params=params(28),
        cost_estimate=cost(15 * 10**9, 4 * 10**6, SEG * SEG),
        name="near_part",
    )(offsets, kv, qg, stat)


def finish_kernel(offs_ref, dq_ref, acc, parts_ref, out_ref):
    offset = offs_ref[lax.axis_index("inner")]
    for b in range(NB):
        start = entry(KV_ORDER, b) * BLOCK
        place = entry(OUT_ORDER, b)
        out_ref[place, :BLOCK, :] = acc[start : start + BLOCK, :].astype(BF)
        out_ref[place, BLOCK:, :] = dq_ref[entry(QG_ORDER, b)]
    start = pl.multiple_of(entry(KV_ORDER, offset) * BLOCK, BLOCK)
    total = acc[pl.ds(start, BLOCK), :]
    for n in range(NB):
        total += parts_ref[n].astype(F32)
    out_ref[entry(OUT_ORDER, offset), :BLOCK, :] = total.astype(BF)


def finish(offsets, dq, sums, parts):
    return pl.pallas_call(
        finish_kernel,
        out_shape=jax.ShapeDtypeStruct((NB, OUT_ROWS, BLOCK), BF),
        in_specs=[SMEM, VMEM, VMEM, VMEM],
        out_specs=VMEM,
        compiler_params=params(16),
        cost_estimate=cost(10**6, 10**6),
        name="finish_picked",
    )(offsets, dq, sums, parts)


def unpack_kernel(in_ref, q_out, k_out, v_out, q_ref, k_ref, v_ref, sems):
    outs = []
    for n in range(GROUPS):
        for pair in range(n * GROUP // 2, (n + 1) * GROUP // 2):
            cols = slice(pair * 2 * HD, (pair + 1) * 2 * HD)
            first, second = (in_ref.at[entry(OUT_ORDER, 2 * pair + n)] for n in range(2))
            one, two = first[:BLOCK, :], second[:BLOCK, :]
            k_ref[:, cols] = jnp.concatenate([one[:, :HD], two[:, :HD]], axis=1)
            v_ref[:, cols] = jnp.concatenate([one[:, HD:], two[:, HD:]], axis=1)
            turned = jnp.concatenate([first[BLOCK:, :], second[BLOCK:, :]], axis=0)
            q_ref[:, cols] = turned.T
        cols = pl.ds(n * GROUP_COLS, GROUP_COLS)
        pairs = [(ref.at[:, cols], out.at[:, cols]) for ref, out in ((q_ref, q_out), (k_ref, k_out), (v_ref, v_out))]
        outs += fetch(pairs, sems.at[n])
    for out in outs:
        out.wait()


def unpack(block):
    shape = jax.ShapeDtypeStruct((BLOCK, HEADS * HD), BF)
    return pl.pallas_call(
        unpack_kernel,
        out_shape=(shape, shape, shape),
        in_specs=[VMEM],
        out_specs=(ANY, ANY, ANY),
        scratch_shapes=[pltpu.VMEM((BLOCK, HEADS * HD), BF)] * 3
        + [pltpu.SemaphoreType.DMA((GROUPS, 3))],
        compiler_params=params(16),
        cost_estimate=cost(10**6, 2 * 10**6),
        name="unpack_heads",
    )(block)


def exchange(array, axis, order=None):
    groups = None
    if order is not None:
        sign, first = order
        groups = [[(first + sign * n) % HEADS for n in range(HEADS)]]
    return lax.all_to_all(
        array, axis, split_axis=0, concat_axis=0, tiled=True, axis_index_groups=groups
    )


def spread(block):
    inner_count = lax.axis_size("inner")

    def ring(step, first):
        pairs = []
        for place in range(RING * RING):
            x, y = place // RING, place % RING
            along_y = x * RING + (y + step) % RING
            along_x = (x + step) % RING * RING + y
            for inner in range(inner_count):
                source = along_y if (inner % 2 == 1) == first else along_x
                pairs.append((source * inner_count + inner, place * inner_count + inner))
        return pairs

    def send(array, step, first):
        return lax.ppermute(array, ("outer", "inner"), ring(step, first))

    row = jnp.stack([block] + [send(block, n, True) for n in (1, 2, 3)])
    return [row] + [send(row, n, False) for n in (1, 2, 3)]


def on_device(queries, keys, values, saved_out, out_grad, offsets):
    kv = exchange(pack_kv(keys, values), "inner", KV_ORDER)
    qg = pack_qg(queries, saved_out, out_grad)
    fars = spread(pick(offsets, kv))
    qg = exchange(qg, "inner", QG_ORDER)
    near_stat = prepare(offsets, kv, qg)
    parts, stat = far_part(offsets, qg, near_stat, fars)
    parts = exchange(parts, "outer")
    dq, sums = near_part(offsets, kv, qg, stat)
    whole = finish(offsets, dq, sums, parts)
    return unpack(exchange(whole, "inner", OUT_ORDER))


def solution(mesh):
    rows = P(("outer", "inner"), None)
    return jax.shard_map(
        on_device,
        mesh=mesh,
        in_specs=(rows, rows, rows, rows, rows, P()),
        out_specs=(rows, rows, rows),
        check_vma=False,
    )
```
